32 devices in a mesh: dp: 8 (over z, core), seq: 4 (over y, x).
Axes of the slice: x: 2, y: 2, z: 4, core: 2. Of those that a mesh axis runs over, the one named last changes fastest.
Arguments:
- first_layer_input: bfloat16 [8, 2048, 1024], P('dp', 'seq'), may hold values from -6 to 6
- cotangent: bfloat16 [8, 2048, 1024], P('dp', 'seq'), may hold values from -6 to 6
- lengths: int32 [8, 16], P('dp'), may hold values from 1 to 1537, 2048 in all within a row
- w_qkv: bfloat16 [2, 1024, 3072], P(None, 'dp'), may hold values from -0.1875 to 0.1875
- bias_qkv: bfloat16 [2, 3072], replicated, may hold values from -3 to 3
- w_out: bfloat16 [2, 1024, 1024], P(None, 'dp'), may hold values from -0.75 to 0.75
- bias_out: bfloat16 [2, 1024], replicated, may hold values from -3 to 3
- w_in: bfloat16 [2, 1024, 4096], P(None, 'dp'), may hold values from -0.1875 to 0.1875
- bias_in: bfloat16 [2, 4096], replicated, may hold values from -3 to 3
- w_back: bfloat16 [2, 4096, 1024], P(None, 'dp'), may hold values from -0.09375 to 0.09375
- bias_back: bfloat16 [2, 1024], replicated, may hold values from -3 to 3
- norm_gain: bfloat16 [2, 2, 1024], replicated, may hold values from 0.5 to 1.5
- norm_shift: bfloat16 [2, 2, 1024], replicated, may hold values from -2 to 2
- prefix_keys: bfloat16 [2, 64, 1024], replicated, may hold values from -6 to 6
- prefix_values: bfloat16 [2, 64, 1024], replicated, may hold values from -6 to 6
Outputs:
- hidden_out: bfloat16 [8, 2048, 1024], P('dp', 'seq')
- input_grad: bfloat16 [8, 2048, 1024], P('dp', 'seq')
- prefix_key_grad: float32 [2, 64, 1024], replicated
- prefix_value_grad: float32 [2, 64, 1024], replicated
The draws below stay inside these ranges and needn't reach their ends.
Inputs may be any that keep to these rules, and one draw needn't show every extreme that they name: The lengths of a row sum to 2048; in every row one pair has exactly 1537 tokens.
All inputs are finite; a program needn't handle non-finite values.
Results may differ from the reference program's by a relative error of at most 0.03.
Values may be sent and summed in bfloat16 or wider, within the bound.
No kernel may reach another device: no remote copies, remote signals or barrier semaphores. Data moves between devices by JAX's collectives and lax.ppermute only.
A program may use at most 576 MiB of HBM per device.

```python
import math
import jax
import jax.numpy as jnp
import numpy as np
from jax import lax

MODEL_WIDTH = 1024
HEADS = 16
HEAD = 64
FF = 4096
PREFIX = 64
LAYERS = 2
PAIRS_PER_ROW = 16
ROW_LENGTH = 2048
DEVICE_TOKENS = 512
PACKED_ROWS = 8


def shard_levels(key, shape, split, smallest, high):
    gain, own = 1.0, jax.random.fold_in(key, 6)
    for axis_at, shards_of in split:
        heights = jnp.exp(jax.random.uniform(jax.random.fold_in(own, axis_at), (shards_of,), jnp.float32, smallest / len(split), high / len(split)))
        gain = gain * jnp.repeat(heights, shape[axis_at] // shards_of).reshape([-1 if axis == axis_at else 1 for axis in range(len(shape))])
    return gain


def split_up(count, total, most, lean):
    portions = [(1 << 20) // math.isqrt(rank ** lean) + 1 for rank in range(2, count + 1)]
    surplus, given = total - most - (count - 1), [1] * (count - 1)
    while surplus > 0:
        movable = [i for i in range(count - 1) if given[i] < most]
        pool, remaining = sum([portions[i] for i in movable]), surplus
        for i in movable:
            extra = min(most - given[i], max(1, remaining * portions[i] // pool), surplus)
            given[i] = given[i] + extra
            surplus = surplus - extra
    return np.array([most] + given)


def uneven(rng, amount, total, limit, skew):
    if amount == 2:
        one = jax.random.randint(rng, (), max(1, total - limit), min(limit, total - 1) + 1)
        return jnp.stack([one, total - one])
    sizes = jnp.asarray(split_up(amount, total, limit, skew), jnp.int32)
    twos = (amount - 1) // 2
    donor, taker = sizes[1:1 + 2 * twos:2], sizes[2:2 + 2 * twos:2]
    room = jnp.minimum(donor - 1, limit - taker)
    passed = jax.random.randint(jax.random.fold_in(rng, 1), (twos,), 0, 1 << 20) % (room + 1)
    sizes = sizes.at[1:1 + 2 * twos:2].set(donor - passed).at[2:2 + 2 * twos:2].set(taker + passed)
    return sizes[jax.random.permutation(jax.random.fold_in(rng, 2), amount)]


def scatter_about(key, shape, deviation, bound, shards=(), held_as=jnp.bfloat16):
    loudness = shard_levels(key, shape, shards, -0.22, 0.18) if shards else 1.0
    result = jax.random.normal(key, shape, jnp.float32) * deviation * loudness
    return jnp.minimum(jnp.maximum(result, -bound), bound).astype(held_as)


def setup_inputs(seed: int = 0) -> dict:
    key_of = jax.random.split(jax.random.key(seed), 16)
    return {
        "first_layer_input": scatter_about(key_of[0], (PACKED_ROWS, ROW_LENGTH, MODEL_WIDTH), 1.0, 6.0, ((0, 8), (1, 4))),
        "cotangent": scatter_about(key_of[1], (PACKED_ROWS, ROW_LENGTH, MODEL_WIDTH), 1.0, 6.0, ((0, 8), (1, 4))),
        "lengths": jax.vmap(lambda own: uneven(own, PAIRS_PER_ROW, ROW_LENGTH, ROW_LENGTH - DEVICE_TOKENS + 1, 2))(jax.random.split(key_of[2], PACKED_ROWS)).reshape((PACKED_ROWS, PAIRS_PER_ROW)).astype(jnp.int32),
        "w_qkv": scatter_about(key_of[3], (LAYERS, MODEL_WIDTH, 3 * MODEL_WIDTH), MODEL_WIDTH ** -0.5, 0.1875, ((1, 8),)),
        "bias_qkv": scatter_about(key_of[4], (LAYERS, 3 * MODEL_WIDTH), 0.5, 3.0),
        "w_out": scatter_about(key_of[5], (LAYERS, MODEL_WIDTH, MODEL_WIDTH), (MODEL_WIDTH // 16) ** -0.5, 0.75, ((1, 8),)),
        "bias_out": scatter_about(key_of[6], (LAYERS, MODEL_WIDTH), 0.5, 3.0),
        "w_in": scatter_about(key_of[7], (LAYERS, MODEL_WIDTH, FF), MODEL_WIDTH ** -0.5, 0.1875, ((1, 8),)),
        "bias_in": scatter_about(key_of[8], (LAYERS, FF), 0.5, 3.0),
        "w_back": scatter_about(key_of[9], (LAYERS, FF, MODEL_WIDTH), FF ** -0.5, 0.09375, ((1, 8),)),
        "bias_back": scatter_about(key_of[10], (LAYERS, MODEL_WIDTH), 0.5, 3.0),
        "norm_gain": jnp.clip(1.0 + 0.1 * jax.random.normal(key_of[11], (LAYERS, 2, MODEL_WIDTH), jnp.float32), 0.5, 1.5).astype(jnp.bfloat16),
        "norm_shift": scatter_about(key_of[12], (LAYERS, 2, MODEL_WIDTH), 0.3, 2.0),
        "prefix_keys": scatter_about(key_of[13], (LAYERS, PREFIX, MODEL_WIDTH), 1.0, 6.0),
        "prefix_values": scatter_about(key_of[14], (LAYERS, PREFIX, MODEL_WIDTH), 1.0, 6.0),
    }


SCALE = 0.125
EPS = 1e-05
HIGHEST = lax.Precision.HIGHEST

@jax.custom_vjp
def low(v):
    return lax.optimization_barrier(v.astype(jnp.bfloat16)).astype(jnp.float32)

@jax.custom_vjp
def low_back(v):
    return v

def low_keep(v):
    return (low(v), None)

def low_pass(kept, grad):
    return (grad,)

def back_keep(v):
    return (v, None)

def back_low(kept, grad):
    return (low(grad),)
low.defvjp(low_keep, low_pass)
low_back.defvjp(back_keep, back_low)

def rounded(values):
    return low_back(low(values))

def layer_norm(values, gain_row, shift_row):
    center = lax.optimization_barrier(jnp.mean(values, -1, keepdims=True))
    centered = values - center
    spread = lax.optimization_barrier(jnp.mean(centered * centered, -1, keepdims=True))
    return centered * lax.rsqrt(spread + EPS) * gain_row + shift_row

def token_segment_codes(pair_lengths, offset_rows, row_count):
    ends_at = jnp.cumsum(pair_lengths, dtype=jnp.int32)
    places = offset_rows + jnp.arange(row_count, dtype=jnp.int32)
    return lax.optimization_barrier(jnp.sum((places[:, None] >= ends_at[None, :]).astype(jnp.int32), 1, dtype=jnp.int32))

def allowed(query_codes, key_codes):
    return query_codes[:, None] == key_codes[None, :]

def attention(queries, keys, values, segment_codes, prefix_keys, prefix_values):
    row_count = queries.shape[0]
    block = math.gcd(row_count, 512)
    prefix_count = prefix_keys.shape[0]
    query_blocks = queries.reshape(row_count // block, block, HEADS, HEAD)
    code_blocks = segment_codes.reshape(row_count // block, block)
    key_rows = jnp.concatenate([prefix_keys.reshape(prefix_count, HEADS, HEAD), keys.reshape(row_count, HEADS, HEAD)], 0)
    value_rows = jnp.concatenate([prefix_values.reshape(prefix_count, HEADS, HEAD), values.reshape(row_count, HEADS, HEAD)], 0)

    def one_block(pieces):
        query_block, code_block = pieces
        scores = jnp.einsum('qhe,khe->hqk', query_block, key_rows, precision=HIGHEST) * SCALE
        scores = low_back(scores)
        visible = jnp.concatenate([jnp.ones((block, prefix_count), jnp.bool_), allowed(code_block, segment_codes)], 1)
        scores = jnp.where(visible[None], scores, -jnp.inf)
        weights = low(jax.nn.softmax(scores, -1))
        return jnp.einsum('hqk,khe->qhe', weights, value_rows, precision=HIGHEST)
    context = lax.map(jax.checkpoint(one_block), (query_blocks, code_blocks))
    return context.reshape(row_count, HEADS * HEAD)

def layer(inputs, segment_codes, weights, prefix_keys, prefix_values):
    w_qkv, bias_qkv, w_out, bias_out, w_in, bias_in, w_back, bias_back, gains, shifts = weights
    projected = jnp.dot(inputs, w_qkv, precision=HIGHEST) + bias_qkv
    queries = rounded(projected[:, :MODEL_WIDTH])
    keys = rounded(projected[:, MODEL_WIDTH:2 * MODEL_WIDTH])
    values = rounded(projected[:, 2 * MODEL_WIDTH:])
    context = rounded(attention(queries, keys, values, segment_codes, prefix_keys, prefix_values))
    branch_one = low_back(jnp.dot(context, w_out, precision=HIGHEST) + bias_out)
    normed = layer_norm(inputs + branch_one, gains[0], shifts[0])
    inner = low_back(jnp.dot(low(normed), w_in, precision=HIGHEST) + bias_in)
    activated = low(jax.nn.gelu(inner, approximate=False))
    branch_two = low_back(jnp.dot(activated, w_back, precision=HIGHEST) + bias_back)
    return layer_norm(normed + branch_two, gains[1], shifts[1])

def reference(first_layer_input, cotangent, lengths, w_qkv, bias_qkv, w_out, bias_out, w_in, bias_in, w_back, bias_back, norm_gain, norm_shift, prefix_keys, prefix_values):
    stacked = [item.astype(jnp.float32) for item in (w_qkv, bias_qkv, w_out, bias_out, w_in, bias_in, w_back, bias_back, norm_gain, norm_shift)]
    segment_codes = jnp.stack([token_segment_codes(lengths[packed_row_index], 0, ROW_LENGTH) for packed_row_index in range(PACKED_ROWS)])

    def forward(inputs, all_prefix_keys, all_prefix_values):

        def one_row(pieces):
            current, row_codes = pieces
            for layer_index in range(LAYERS):
                weights = tuple((item[layer_index] for item in stacked))
                current = layer(current, row_codes, weights, all_prefix_keys[layer_index], all_prefix_values[layer_index])
                if layer_index + 1 < LAYERS:
                    current = low(current)
            return current
        return lax.map(jax.checkpoint(one_row), (inputs, segment_codes))
    outputs, pull_back = jax.vjp(forward, first_layer_input.astype(jnp.float32), prefix_keys.astype(jnp.float32), prefix_values.astype(jnp.float32))
    grad_in, grad_keys, grad_values = pull_back(cotangent.astype(jnp.float32))
    return (outputs.astype(jnp.bfloat16), grad_in.astype(jnp.bfloat16), grad_keys, grad_values)
```

```python
import jax
import jax.numpy as jnp
from jax import lax
from jax.sharding import PartitionSpec as P

HEADS = 16
HEAD = 64


SCALE = 0.125
EPS = 1e-05


def layer_norm(values, gain_row, shift_row):
    center = jnp.mean(values, -1, keepdims=True)
    centered = values - center
    spread = jnp.mean(centered * centered, -1, keepdims=True)
    return centered * lax.rsqrt(spread + EPS) * gain_row + shift_row


def smooth(values):
    return jax.nn.gelu(values, approximate=False)


def back_dot(left, right):
    return lax.dot_general(
        left, right, (((1,), (1,)), ((), ())), preferred_element_type=jnp.float32
    )


def token_segment_codes(pair_lengths, offset_rows, row_count):
    pair_at = jnp.arange(pair_lengths.shape[0], dtype=jnp.int32)
    ends_at = jnp.sum(
        jnp.where(pair_at[:, None] <= pair_at[None, :], pair_lengths[:, None], 0), 0, dtype=jnp.int32
    )
    places = offset_rows + jnp.arange(row_count, dtype=jnp.int32)
    return jnp.sum((places[:, None] >= ends_at[None, :]).astype(jnp.int32), 1, dtype=jnp.int32)


def allowed(query_codes, key_codes):
    return query_codes[:, None] == key_codes[None, :]


def heads_of(values):
    return values.reshape(values.shape[0], HEADS, HEAD)


def attend_forward(queries, keys, values, segment_codes, prefix_heads, prefix_value_heads):
    query_heads = heads_of(queries)
    prefix_scores = (
        jnp.einsum("qhe,khe->hqk", query_heads, prefix_heads, preferred_element_type=jnp.float32)
        * SCALE
    )
    running_top = jnp.max(prefix_scores, -1)
    prefix_weights = jnp.exp(prefix_scores - running_top[..., None])
    running_sum = jnp.sum(prefix_weights, -1)
    running_acc = jnp.einsum(
        "hqk,khe->hqe",
        prefix_weights.astype(jnp.bfloat16),
        prefix_value_heads,
        preferred_element_type=jnp.float32,
    )
    key_piece = lax.all_gather(keys, "seq", axis=0, tiled=True)
    value_piece = lax.all_gather(values, "seq", axis=0, tiled=True)
    code_piece = lax.all_gather(segment_codes, "seq", axis=0, tiled=True)
    scores = (
        jnp.einsum(
            "qhe,khe->hqk", query_heads, heads_of(key_piece), preferred_element_type=jnp.float32
        )
        * SCALE
    )
    scores = jnp.where(allowed(segment_codes, code_piece)[None], scores, -jnp.inf)
    new_top = jnp.maximum(running_top, jnp.max(scores, -1))
    factor = jnp.exp(running_top - new_top)
    weights = jnp.exp(scores - new_top[..., None])
    new_sum = running_sum * factor + jnp.sum(weights, -1)
    new_acc = running_acc * factor[..., None] + jnp.einsum(
        "hqk,khe->hqe",
        weights.astype(jnp.bfloat16),
        heads_of(value_piece),
        preferred_element_type=jnp.float32,
    )
    context = new_acc / new_sum[..., None]
    context = jnp.transpose(context, (1, 0, 2)).reshape(queries.shape[0], HEADS * HEAD)
    log_total = jnp.transpose(new_top + jnp.log(new_sum))
    return (context, log_total)


def attend_backward(
    queries,
    keys,
    values,
    segment_codes,
    prefix_heads,
    prefix_value_heads,
    log_total,
    delta_rows,
    grad_context,
):
    query_heads = heads_of(queries)
    grad_heads = heads_of(grad_context)
    log_heads = jnp.transpose(log_total)[..., None]
    delta_heads = jnp.transpose(delta_rows)[..., None]
    prefix_scores = (
        jnp.einsum("qhe,khe->hqk", query_heads, prefix_heads, preferred_element_type=jnp.float32)
        * SCALE
    )
    prefix_prob = jnp.exp(prefix_scores - log_heads)
    prefix_dprob = jnp.einsum(
        "qhe,khe->hqk", grad_heads, prefix_value_heads, preferred_element_type=jnp.float32
    )
    prefix_dscore = (prefix_prob * (prefix_dprob - delta_heads)).astype(jnp.bfloat16)
    grad_query = (
        jnp.einsum("hqk,khe->qhe", prefix_dscore, prefix_heads, preferred_element_type=jnp.float32)
        * SCALE
    )
    grad_prefix_key = (
        jnp.einsum("hqk,qhe->khe", prefix_dscore, query_heads, preferred_element_type=jnp.float32)
        * SCALE
    )
    grad_prefix_value = jnp.einsum(
        "hqk,qhe->khe",
        prefix_prob.astype(jnp.bfloat16),
        grad_heads,
        preferred_element_type=jnp.float32,
    )
    key_piece = lax.all_gather(keys, "seq", axis=0, tiled=True)
    value_piece = lax.all_gather(values, "seq", axis=0, tiled=True)
    code_piece = lax.all_gather(segment_codes, "seq", axis=0, tiled=True)
    query_key_heads = heads_of(key_piece)
    scores = (
        jnp.einsum("qhe,khe->hqk", query_heads, query_key_heads, preferred_element_type=jnp.float32)
        * SCALE
    )
    scores = jnp.where(allowed(segment_codes, code_piece)[None], scores, -jnp.inf)
    prob = jnp.exp(scores - log_heads)
    dprob = jnp.einsum(
        "qhe,khe->hqk", grad_heads, heads_of(value_piece), preferred_element_type=jnp.float32
    )
    dscore = (prob * (dprob - delta_heads)).astype(jnp.bfloat16)
    grad_query = (
        grad_query
        + jnp.einsum("hqk,khe->qhe", dscore, query_key_heads, preferred_element_type=jnp.float32)
        * SCALE
    )
    key_heads = heads_of(keys)
    value_heads = heads_of(values)
    query_piece = lax.all_gather(queries, "seq", axis=0, tiled=True)
    grad_piece = lax.all_gather(grad_context, "seq", axis=0, tiled=True)
    log_piece = lax.all_gather(log_total.astype(jnp.bfloat16), "seq", axis=0, tiled=True).astype(
        jnp.float32
    )
    delta_piece = lax.all_gather(delta_rows.astype(jnp.bfloat16), "seq", axis=0, tiled=True).astype(
        jnp.float32
    )
    code_piece = lax.all_gather(segment_codes, "seq", axis=0, tiled=True)
    piece_heads = heads_of(query_piece)
    piece_grads = heads_of(grad_piece)
    scores = (
        jnp.einsum("qhe,khe->hqk", piece_heads, key_heads, preferred_element_type=jnp.float32)
        * SCALE
    )
    scores = jnp.where(allowed(code_piece, segment_codes)[None], scores, -jnp.inf)
    prob = jnp.exp(scores - jnp.transpose(log_piece)[..., None])
    dprob = jnp.einsum("qhe,khe->hqk", piece_grads, value_heads, preferred_element_type=jnp.float32)
    dscore = (prob * (dprob - jnp.transpose(delta_piece)[..., None])).astype(jnp.bfloat16)
    grad_key_part = (
        jnp.einsum("hqk,qhe->khe", dscore, piece_heads, preferred_element_type=jnp.float32) * SCALE
    )
    grad_value_part = jnp.einsum(
        "hqk,qhe->khe", prob.astype(jnp.bfloat16), piece_grads, preferred_element_type=jnp.float32
    )
    return (grad_query, grad_key_part, grad_value_part, grad_prefix_key, grad_prefix_value)


def local(
    first_layer_input,
    cotangent,
    lengths,
    w_qkv,
    bias_qkv,
    w_out,
    bias_out,
    w_in,
    bias_in,
    w_back,
    bias_back,
    norm_gain,
    norm_shift,
    prefix_keys,
    prefix_values,
):
    row_count = first_layer_input.shape[1]
    width = first_layer_input.shape[2]
    layer_count = w_qkv.shape[0]
    offset_rows = lax.axis_index("seq") * row_count
    segment_codes = token_segment_codes(lengths[0], offset_rows, row_count)
    current = first_layer_input[0]
    saved = []
    gathered = []
    for layer_index in range(layer_count):
        matrices = (
            lax.all_gather(w_qkv[layer_index], "dp", axis=0, tiled=True),
            lax.all_gather(w_out[layer_index], "dp", axis=0, tiled=True),
            lax.all_gather(w_in[layer_index], "dp", axis=0, tiled=True),
            lax.all_gather(w_back[layer_index], "dp", axis=0, tiled=True),
        )
        gathered.append(matrices)
        mat_qkv, mat_out, mat_in, mat_back = matrices
        prefix_heads = heads_of(prefix_keys[layer_index])
        prefix_value_heads = heads_of(prefix_values[layer_index])
        gains = norm_gain[layer_index].astype(jnp.float32)
        shifts = norm_shift[layer_index].astype(jnp.float32)
        projected = jnp.dot(current, mat_qkv, preferred_element_type=jnp.float32) + bias_qkv[
            layer_index
        ].astype(jnp.float32)
        queries = projected[:, :width].astype(jnp.bfloat16)
        keys = projected[:, width : 2 * width].astype(jnp.bfloat16)
        values = projected[:, 2 * width :].astype(jnp.bfloat16)
        context, log_total = attend_forward(
            queries, keys, values, segment_codes, prefix_heads, prefix_value_heads
        )
        residual_one = (
            current.astype(jnp.float32)
            + jnp.dot(context.astype(jnp.bfloat16), mat_out, preferred_element_type=jnp.float32)
            + bias_out[layer_index].astype(jnp.float32)
        )
        normed = layer_norm(residual_one, gains[0], shifts[0])
        inner = jnp.dot(
            normed.astype(jnp.bfloat16), mat_in, preferred_element_type=jnp.float32
        ) + bias_in[layer_index].astype(jnp.float32)
        activated = smooth(inner).astype(jnp.bfloat16)
        residual_two = (
            normed
            + jnp.dot(activated, mat_back, preferred_element_type=jnp.float32)
            + bias_back[layer_index].astype(jnp.float32)
        )
        result = layer_norm(residual_two, gains[1], shifts[1])
        saved.append((queries, keys, values, context, log_total, residual_one, inner, residual_two))
        current = result.astype(jnp.bfloat16)
    gradient = cotangent[0].astype(jnp.float32)
    key_grads = []
    value_grads = []
    for layer_index in reversed(range(layer_count)):
        queries, keys, values, context, log_total, residual_one, inner, residual_two = saved[
            layer_index
        ]
        mat_qkv, mat_out, mat_in, mat_back = (
            lax.all_gather(w_qkv[layer_index], "dp", axis=0, tiled=True),
            lax.all_gather(w_out[layer_index], "dp", axis=0, tiled=True),
            lax.all_gather(w_in[layer_index], "dp", axis=0, tiled=True),
            lax.all_gather(w_back[layer_index], "dp", axis=0, tiled=True),
        )
        prefix_heads = heads_of(prefix_keys[layer_index])
        prefix_value_heads = heads_of(prefix_values[layer_index])
        gains = norm_gain[layer_index].astype(jnp.float32)
        shifts = norm_shift[layer_index].astype(jnp.float32)
        unused_two, pull_two = jax.vjp(
            lambda rows: layer_norm(rows, gains[1], shifts[1]), residual_two
        )
        (grad_two,) = pull_two(gradient)
        grad_hidden = back_dot(grad_two.astype(jnp.bfloat16), mat_back)
        unused_inner, pull_smooth = jax.vjp(smooth, inner)
        (grad_inner,) = pull_smooth(grad_hidden)
        grad_normed = grad_two + back_dot(grad_inner.astype(jnp.bfloat16), mat_in)
        unused_one, pull_one = jax.vjp(
            lambda rows: layer_norm(rows, gains[0], shifts[0]), residual_one
        )
        (grad_one,) = pull_one(grad_normed)
        grad_context = back_dot(grad_one.astype(jnp.bfloat16), mat_out).astype(jnp.bfloat16)
        delta_rows = jnp.sum(heads_of(grad_context.astype(jnp.float32) * context), -1)
        grad_query, grad_key, grad_value, grad_prefix_key, grad_prefix_value = attend_backward(
            queries,
            keys,
            values,
            segment_codes,
            prefix_heads,
            prefix_value_heads,
            log_total,
            delta_rows,
            grad_context,
        )
        grad_prefix_key = grad_prefix_key.reshape(grad_prefix_key.shape[0], width)
        grad_prefix_value = grad_prefix_value.reshape(grad_prefix_value.shape[0], width)
        grad_prefix_key, grad_prefix_value = lax.psum(
            (grad_prefix_key, grad_prefix_value), ("dp", "seq")
        )
        key_grads.append(grad_prefix_key)
        value_grads.append(grad_prefix_value)
        grad_projected = jnp.concatenate(
            [
                grad_query.reshape(row_count, width),
                grad_key.reshape(row_count, width),
                grad_value.reshape(row_count, width),
            ],
            1,
        ).astype(jnp.bfloat16)
        gradient = grad_one + back_dot(grad_projected, mat_qkv)
    key_stack = jnp.stack(key_grads[::-1])
    value_stack = jnp.stack(value_grads[::-1])
    return (current[None], gradient.astype(jnp.bfloat16)[None], key_stack, value_stack)


def solution(mesh):
    in_specs = (
        P("dp", "seq", None),
        P("dp", "seq", None),
        P("dp", None),
        P(None, "dp", None),
        P(),
        P(None, "dp", None),
        P(),
        P(None, "dp", None),
        P(),
        P(None, "dp", None),
        P(),
        P(),
        P(),
        P(),
        P(),
    )
    out_specs = (P("dp", "seq", None), P("dp", "seq", None), P(), P())
    return jax.shard_map(local, mesh=mesh, in_specs=in_specs, out_specs=out_specs, check_vma=False)
```

```python
import functools
import math

import jax
import jax.numpy as jnp
from jax import lax
from jax.experimental import pallas as pl
from jax.experimental.pallas import tpu as pltpu
from jax.sharding import PartitionSpec as P

HEADS = 16
HEAD = 64

SCALE = 0.125
LOG2_E = math.log2(math.e)
LN_2 = math.log(2.0)
EPS = 1e-05
BLOCK = 256
VMEM_BYTES = 48 * 2**20


def dot(left, right):
    return jnp.dot(left, right, preferred_element_type=jnp.float32)


def back_dot(left, right):
    return lax.dot_general(
        left, right, (((1,), (1,)), ((), ())), preferred_element_type=jnp.float32
    )


def normalize(values):
    center = jnp.mean(values, -1, keepdims=True)
    centered = values - center
    spread = jnp.mean(centered * centered, -1, keepdims=True)
    inverse = lax.rsqrt(spread + EPS)
    return centered * inverse, inverse


def normalize_back(gradient, normal, inverse, gain_row):
    scaled = gradient * gain_row
    first = jnp.mean(scaled, -1, keepdims=True)
    second = jnp.mean(scaled * normal, -1, keepdims=True)
    return (scaled - first - normal * second) * inverse


def gelu_pair(inner):
    bell = jnp.exp(inner * inner * -0.5)
    phi = 0.5 + 0.5 * lax.erf(inner * (0.5**0.5))
    return inner * phi, phi + inner * bell * ((2.0 * math.pi) ** -0.5)


def head_rows(step_heads, head, block):
    if step_heads == 1:
        return block
    parts = [
        block[other * HEAD : (other + 1) * HEAD]
        if other == head
        else jnp.zeros((HEAD, block.shape[1]), block.dtype)
        for other in range(step_heads)
    ]
    return jnp.concatenate(parts, 0)


def same_pair(code_columns, code_row):
    columns = jnp.concatenate([code_columns] * (code_row.shape[1] // code_columns.shape[1]), 1)
    return columns == code_row


def forward_kernel(
    step_heads,
    low_ref,
    high_ref,
    q_ref,
    k_ref,
    v_ref,
    pk_ref,
    pv_ref,
    columns_ref,
    row_ref,
    context_ref,
    turned_ref,
    total_ref,
    q_turned,
    v_turned,
):
    blocks = q_ref.shape[0] // BLOCK
    q_turned[...] = q_ref[...].T
    v_turned[...] = v_ref[...].T
    prefix_turned = pv_ref[...].T

    def query_step(i, carry):
        at = pl.ds(pl.multiple_of(i * BLOCK, BLOCK), BLOCK)
        code_row = row_ref[:, at]
        q_block = q_turned[:, at]
        rows = [head_rows(step_heads, h, q_block) for h in range(step_heads)]
        state = []
        for h in range(step_heads):
            scores = dot(pk_ref[...], rows[h])
            top = jnp.max(scores, 0, keepdims=True)
            weights = jnp.exp2(scores - top)
            total = jnp.sum(weights, 0, keepdims=True)
            values = prefix_turned[h * HEAD : (h + 1) * HEAD]
            state.append((top, total, dot(values, weights.astype(jnp.bfloat16))))

        def key_step(j, state):
            place = pl.ds(pl.multiple_of(j * BLOCK, BLOCK), BLOCK)
            keys = k_ref[place, :]
            seen = same_pair(columns_ref[place, :], code_row)
            result = []
            for h in range(step_heads):
                top, total, summed = state[h]
                scores = jnp.where(seen, dot(keys, rows[h]), -jnp.inf)
                new_top = jnp.maximum(top, jnp.max(scores, 0, keepdims=True))
                factor = jnp.exp2(top - new_top)
                weights = jnp.exp2(scores - new_top)
                total = total * factor + jnp.sum(weights, 0, keepdims=True)
                values = v_turned[h * HEAD : (h + 1) * HEAD, place]
                summed = summed * factor + dot(values, weights.astype(jnp.bfloat16))
                result.append((new_top, total, summed))
            return tuple(result)

        state = lax.fori_loop(low_ref[i], high_ref[i], key_step, tuple(state))
        parts = []
        for h in range(step_heads):
            top, total, summed = state[h]
            parts.append(summed / total)
            total_ref[0, h : h + 1, at] = top + jnp.log2(total)
        turned = parts[0] if step_heads == 1 else jnp.concatenate(parts, 0)
        turned_ref[:, at] = turned
        context_ref[at, :] = turned.T.astype(jnp.bfloat16)
        return carry

    lax.fori_loop(0, blocks, query_step, 0)


def backward_kernel(
    step_heads,
    low_ref,
    high_ref,
    q_ref,
    k_ref,
    v_ref,
    g_ref,
    pk_ref,
    pv_ref,
    turned_ref,
    total_ref,
    columns_ref,
    row_ref,
    grads_ref,
    pk_grad_ref,
    pv_grad_ref,
    q_turned,
    g_turned,
    q_alone,
    g_alone,
    k_turned,
    q_sum,
    delta_ref,
    k_sum,
    v_sum,
    pk_sum,
    pv_sum,
):
    row_count, width = q_ref.shape
    blocks = row_count // BLOCK
    q_all = q_ref[...].T
    g_all = g_ref[...].T
    k_turned[...] = k_ref[...].T
    prefix_turned = pk_ref[...].T
    lane = lax.broadcasted_iota(jnp.int32, (1, width), 1)
    for h in range(step_heads):
        q_turned[h] = head_rows(step_heads, h, q_all)
        g_turned[h] = head_rows(step_heads, h, g_all)
        own = (lane // HEAD == h).astype(jnp.bfloat16)
        q_alone[h] = q_ref[...] * own
        g_alone[h] = g_ref[...] * own
        part = slice(h * HEAD, (h + 1) * HEAD)
        delta_ref[h : h + 1, :] = jnp.sum(
            g_all[part].astype(jnp.float32) * turned_ref[part, :], 0, keepdims=True
        )
    q_sum[...] = jnp.zeros_like(q_sum)
    pk_sum[...] = jnp.zeros_like(pk_sum)
    pv_sum[...] = jnp.zeros_like(pv_sum)

    def pair_of_blocks(i, keys, values, keys_turned, seen, key_total, value_total):
        at = pl.ds(pl.multiple_of(i * BLOCK, BLOCK), BLOCK)
        if seen is not None:
            seen = same_pair(seen, row_ref[:, at])
        for h in range(step_heads):
            part = slice(h * HEAD, (h + 1) * HEAD)
            scores = dot(keys, q_turned[h, :, at])
            weights = jnp.exp2(scores - total_ref[0, h : h + 1, at])
            if seen is not None:
                weights = jnp.where(seen, weights, 0.0)
            grad_weights = dot(values, g_turned[h, :, at])
            grad_scores = (weights * (grad_weights - delta_ref[h : h + 1, at])).astype(jnp.bfloat16)
            value_total[...] += dot(weights.astype(jnp.bfloat16), g_alone[h, at, :])
            key_total[...] += dot(grad_scores, q_alone[h, at, :])
            q_sum[part, at] += dot(keys_turned[part, :], grad_scores)

    def prefix_step(i, carry):
        pair_of_blocks(i, pk_ref[...], pv_ref[...], prefix_turned, None, pk_sum, pv_sum)
        return carry

    lax.fori_loop(0, blocks, prefix_step, 0)
    pk_grad_ref[...] = pk_sum[...] * LN_2
    pv_grad_ref[...] = pv_sum[...]

    def key_step(j, carry):
        place = pl.ds(pl.multiple_of(j * BLOCK, BLOCK), BLOCK)
        k_sum[...] = jnp.zeros_like(k_sum)
        v_sum[...] = jnp.zeros_like(v_sum)
        keys, values = k_ref[place, :], v_ref[place, :]
        keys_turned = k_turned[:, place]
        seen = columns_ref[place, :]

        def query_step(i, carry):
            pair_of_blocks(i, keys, values, keys_turned, seen, k_sum, v_sum)
            return carry

        lax.fori_loop(low_ref[j], high_ref[j], query_step, 0)
        grads_ref[1, place, :] = (k_sum[...] * LN_2).astype(jnp.bfloat16)
        grads_ref[2, place, :] = v_sum[...].astype(jnp.bfloat16)
        return carry

    lax.fori_loop(0, blocks, key_step, 0)
    grads_ref[0] = (q_sum[...] * SCALE).T.astype(jnp.bfloat16)


def attend(queries, keys, values, prefix_k, prefix_v, low, high, columns, row):
    rows, width = queries.shape
    step_heads = 2 if width % (2 * HEAD) == 0 else 1
    part = step_heads * HEAD
    steps = width // part
    prefix = prefix_k.shape[0]
    whole = pl.BlockSpec((rows, part), lambda p, *_: (0, p))
    few = pl.BlockSpec((prefix, part), lambda p, *_: (0, p))
    return pl.pallas_call(
        functools.partial(forward_kernel, step_heads),
        grid_spec=pltpu.PrefetchScalarGridSpec(
            num_scalar_prefetch=2,
            grid=(steps,),
            in_specs=[
                whole,
                whole,
                whole,
                few,
                few,
                pl.BlockSpec(columns.shape, lambda p, *_: (0, 0)),
                pl.BlockSpec(row.shape, lambda p, *_: (0, 0)),
            ],
            out_specs=[
                whole,
                pl.BlockSpec((part, rows), lambda p, *_: (p, 0)),
                pl.BlockSpec((1, 8, rows), lambda p, *_: (p, 0, 0)),
            ],
            scratch_shapes=[pltpu.VMEM((part, rows), jnp.bfloat16)] * 2,
        ),
        out_shape=[
            jax.ShapeDtypeStruct((rows, width), jnp.bfloat16),
            jax.ShapeDtypeStruct((width, rows), jnp.float32),
            jax.ShapeDtypeStruct((steps, 8, rows), jnp.float32),
        ],
        compiler_params=pltpu.CompilerParams(vmem_limit_bytes=VMEM_BYTES),
        name="attend",
    )(low, high, queries, keys, values, prefix_k, prefix_v, columns, row)


def attend_back(
    queries, keys, values, grads, prefix_k, prefix_v, turned, total, low, high, columns, row
):
    rows, width = queries.shape
    step_heads = 2 if width % (2 * HEAD) == 0 else 1
    part = step_heads * HEAD
    steps = width // part
    prefix = prefix_k.shape[0]
    whole = pl.BlockSpec((rows, part), lambda p, *_: (0, p))
    few = pl.BlockSpec((prefix, part), lambda p, *_: (0, p))
    return pl.pallas_call(
        functools.partial(backward_kernel, step_heads),
        grid_spec=pltpu.PrefetchScalarGridSpec(
            num_scalar_prefetch=2,
            grid=(steps,),
            in_specs=[
                whole,
                whole,
                whole,
                whole,
                few,
                few,
                pl.BlockSpec((part, rows), lambda p, *_: (p, 0)),
                pl.BlockSpec((1, 8, rows), lambda p, *_: (p, 0, 0)),
                pl.BlockSpec(columns.shape, lambda p, *_: (0, 0)),
                pl.BlockSpec(row.shape, lambda p, *_: (0, 0)),
            ],
            out_specs=[
                pl.BlockSpec((3, rows, part), lambda p, *_: (0, 0, p)),
                few,
                few,
            ],
            scratch_shapes=[
                pltpu.VMEM((step_heads, part, rows), jnp.bfloat16),
                pltpu.VMEM((step_heads, part, rows), jnp.bfloat16),
                pltpu.VMEM((step_heads, rows, part), jnp.bfloat16),
                pltpu.VMEM((step_heads, rows, part), jnp.bfloat16),
                pltpu.VMEM((part, rows), jnp.bfloat16),
                pltpu.VMEM((part, rows), jnp.float32),
                pltpu.VMEM((8, rows), jnp.float32),
                pltpu.VMEM((BLOCK, part), jnp.float32),
                pltpu.VMEM((BLOCK, part), jnp.float32),
                pltpu.VMEM((prefix, part), jnp.float32),
                pltpu.VMEM((prefix, part), jnp.float32),
            ],
        ),
        out_shape=[
            jax.ShapeDtypeStruct((3, rows, width), jnp.bfloat16),
            jax.ShapeDtypeStruct((prefix, width), jnp.float32),
            jax.ShapeDtypeStruct((prefix, width), jnp.float32),
        ],
        compiler_params=pltpu.CompilerParams(vmem_limit_bytes=VMEM_BYTES),
        name="attend_back",
    )(
        low,
        high,
        queries,
        keys,
        values,
        grads,
        prefix_k,
        prefix_v,
        turned,
        total,
        columns,
        row,
    )


def local(
    dp_count,
    seq_count,
    first_layer_input,
    cotangent,
    lengths,
    w_qkv,
    bias_qkv,
    w_out,
    bias_out,
    w_in,
    bias_in,
    w_back,
    bias_back,
    norm_gain,
    norm_shift,
    prefix_keys,
    prefix_values,
):
    row_count = first_layer_input.shape[1]
    width = first_layer_input.shape[2]
    layer_count = w_qkv.shape[0]
    all_rows = row_count * seq_count
    own_width = width // seq_count
    me = lax.axis_index("seq")

    def swap(value, step):
        if step == 0:
            return value
        return lax.ppermute(value, "seq", [(i, i ^ step) for i in range(seq_count)])

    def partner(step):
        return me ^ step

    def spread(matrix):
        share = matrix.shape[0] // seq_count
        piece = lax.dynamic_slice_in_dim(matrix, me * share, share, 0)
        return lax.all_gather(piece, ("dp", "seq"), axis=0, tiled=True)

    def own_columns(values, axis):
        return lax.dynamic_slice_in_dim(values, me * own_width, own_width, axis)

    pair_at = jnp.arange(lengths.shape[1], dtype=jnp.int32)
    ends = jnp.sum(
        jnp.where(pair_at[:, None] <= pair_at[None, :], lengths[0][:, None], 0), 0, dtype=jnp.int32
    )
    starts = ends - lengths[0]
    places = jnp.arange(all_rows, dtype=jnp.int32)
    codes = jnp.sum((places[:, None] >= ends[None, :]).astype(jnp.int32), 1, dtype=jnp.int32)
    columns = jnp.broadcast_to(codes[:, None], (all_rows, 128))
    row = codes[None, :]
    first = jnp.arange(all_rows // BLOCK, dtype=jnp.int32) * BLOCK
    after = first + BLOCK
    low = jnp.max(jnp.where(starts[None, :] <= first[:, None], starts[None, :], 0), 1) // BLOCK
    high = jnp.min(jnp.where(ends[None, :] >= after[:, None], ends[None, :], all_rows), 1)
    high = (high + BLOCK - 1) // BLOCK

    def in_swap_order(blocks, axis):
        return jnp.concatenate(
            [
                lax.dynamic_slice_in_dim(blocks, partner(step), 1, axis)
                for step in range(seq_count)
            ],
            axis,
        )

    current = first_layer_input[0]
    saved = []
    for layer in range(layer_count):
        gains = norm_gain[layer].astype(jnp.float32)
        shifts = norm_shift[layer].astype(jnp.float32)
        shard = w_qkv[layer].reshape(-1, 3, width)
        mat_own = lax.all_gather(
            own_columns(shard, 2).reshape(-1, 3 * own_width), "dp", axis=0, tiled=True
        )
        mat_out = spread(w_out[layer])
        mat_in = spread(w_in[layer])
        mat_back = spread(w_back[layer])
        out_blocks = in_swap_order(mat_out.reshape(seq_count, own_width, width), 0)
        mat_out = out_blocks.reshape(width, width)
        bias_own = own_columns(bias_qkv[layer].reshape(3, width).astype(jnp.float32), 1)
        prefix_k = own_columns(prefix_keys[layer], 1)
        prefix_v = own_columns(prefix_values[layer], 1)

        tokens = jnp.zeros((all_rows, width), jnp.bfloat16)
        for step in range(seq_count):
            tokens = lax.dynamic_update_slice_in_dim(
                tokens, swap(current, step), partner(step) * row_count, 0
            )
        projected = [
            dot(tokens, mat_own[:, n * own_width : (n + 1) * own_width]) + bias_own[n]
            for n in range(3)
        ]
        queries = (projected[0] * (SCALE * LOG2_E)).astype(jnp.bfloat16)
        keys = projected[1].astype(jnp.bfloat16)
        values = projected[2].astype(jnp.bfloat16)
        context, turned, total = attend(
            queries, keys, values, prefix_k, prefix_v, low, high, columns, row
        )
        pieces = [
            swap(
                lax.dynamic_slice_in_dim(context, partner(step) * row_count, row_count, 0), step
            )
            for step in range(seq_count)
        ]
        residual_one = (
            current.astype(jnp.float32)
            + dot(jnp.concatenate(pieces, 1), mat_out)
            + bias_out[layer].astype(jnp.float32)
        )
        normal_one, inverse_one = normalize(residual_one)
        normed = normal_one * gains[0] + shifts[0]
        inner = dot(normed.astype(jnp.bfloat16), mat_in) + bias_in[layer].astype(jnp.float32)
        activated, slope = gelu_pair(inner)
        slope = slope.astype(jnp.bfloat16)
        residual_two = (
            normed
            + dot(activated.astype(jnp.bfloat16), mat_back)
            + bias_back[layer].astype(jnp.float32)
        )
        normal_two, inverse_two = normalize(residual_two)
        result = normal_two * gains[1] + shifts[1]
        current = result.astype(jnp.bfloat16)
        saved.append(
            (
                (queries, keys, values, prefix_k, prefix_v, turned, total),
                (normal_one, inverse_one, slope, normal_two, inverse_two),
                (mat_out, mat_in, mat_back),
            )
        )

    gradient = cotangent[0].astype(jnp.float32)
    prefix_grads = []
    for layer in reversed(range(layer_count)):
        heads, norms, matrices = saved[layer]
        queries, keys, values, prefix_k, prefix_v, turned, total = heads
        normal_one, inverse_one, slope, normal_two, inverse_two = norms
        mat_out, mat_in, mat_back = matrices
        mat_qkv = spread(w_qkv[layer])
        qkv_blocks = in_swap_order(mat_qkv.reshape(width, 3, seq_count, own_width), 2)
        gains = norm_gain[layer].astype(jnp.float32)
        grad_two = normalize_back(gradient, normal_two, inverse_two, gains[1])
        grad_inner = back_dot(grad_two.astype(jnp.bfloat16), mat_back) * slope.astype(jnp.float32)
        grad_normed = grad_two + back_dot(grad_inner.astype(jnp.bfloat16), mat_in)
        grad_one = normalize_back(grad_normed, normal_one, inverse_one, gains[0])
        grad_context = back_dot(grad_one.astype(jnp.bfloat16), mat_out).astype(jnp.bfloat16)
        grads = jnp.zeros((all_rows, own_width), jnp.bfloat16)
        for step in range(seq_count):
            piece = grad_context[:, step * own_width : (step + 1) * own_width]
            grads = lax.dynamic_update_slice_in_dim(
                grads, swap(piece, step), partner(step) * row_count, 0
            )
        grad_heads, pk_grad, pv_grad = attend_back(
            queries, keys, values, grads, prefix_k, prefix_v, turned, total, low, high, columns, row
        )
        prefix_grads.append(jnp.stack([pk_grad, pv_grad]))
        gradient = grad_one
        for step in range(seq_count):
            piece = swap(
                lax.dynamic_slice_in_dim(grad_heads, partner(step) * row_count, row_count, 1), step
            )
            for n in range(3):
                gradient = gradient + back_dot(piece[n], qkv_blocks[:, n, step])

    def everywhere(share):
        stride = 1
        while stride < dp_count:
            share = share + lax.ppermute(share, "dp", [(i, i ^ stride) for i in range(dp_count)])
            stride *= 2
        return lax.all_gather(share, "seq", axis=2, tiled=True)

    sums = [everywhere(item) for item in prefix_grads[::-1]]
    key_stack = jnp.stack([item[0] for item in sums])
    value_stack = jnp.stack([item[1] for item in sums])
    return (current[None], gradient.astype(jnp.bfloat16)[None], key_stack, value_stack)


def solution(mesh):
    in_specs = (
        P("dp", "seq", None),
        P("dp", "seq", None),
        P("dp", None),
        P(None, "dp", None),
        P(),
        P(None, "dp", None),
        P(),
        P(None, "dp", None),
        P(),
        P(None, "dp", None),
        P(),
        P(),
        P(),
        P(),
        P(),
    )
    out_specs = (P("dp", "seq", None), P("dp", "seq", None), P(), P())
    return jax.shard_map(
        functools.partial(local, mesh.shape["dp"], mesh.shape["seq"]),
        mesh=mesh,
        in_specs=in_specs,
        out_specs=out_specs,
        check_vma=False,
    )
```

```python
import functools
import math

import jax
import jax.numpy as jnp
from jax import lax
from jax.experimental import pallas as pl
from jax.experimental.pallas import tpu as pltpu
from jax.sharding import PartitionSpec as P

HEAD = 64

SCALE = 0.125
LOG2_E = math.log2(math.e)
LN_2 = math.log(2.0)
EPS = 1e-05
BLOCK = 256
VMEM_BYTES = 56 * 2**20
FLOPS_A_MICRO = 1.1e9


def dot(left, right):
    return jnp.dot(left, right, preferred_element_type=jnp.float32)


def back_dot(left, right):
    return lax.dot_general(
        left, right, (((1,), (1,)), ((), ())), preferred_element_type=jnp.float32
    )


def normalize(values):
    center = jnp.mean(values, -1, keepdims=True)
    centered = values - center
    spread = jnp.mean(centered * centered, -1, keepdims=True)
    inverse = lax.rsqrt(spread + EPS)
    return centered * inverse, inverse


def normalize_back(gradient, normal, inverse, gain_row):
    scaled = gradient * gain_row
    first = jnp.mean(scaled, -1, keepdims=True)
    second = jnp.mean(scaled * normal, -1, keepdims=True)
    return (scaled - first - normal * second) * inverse


def gelu_pair(inner):
    size = jnp.abs(inner)
    bell = jnp.exp2(inner * inner * (-0.5 * LOG2_E))
    t = 1.0 / (1.0 + (0.3275911 * 0.5**0.5) * size)
    tail = 0.5 * 1.061405429
    for factor in (-1.453152027, 1.421413741, -0.284496736, 0.254829592):
        tail = tail * t + 0.5 * factor
    tail = tail * t * bell
    phi = jnp.where(inner >= 0.0, 1.0 - tail, tail)
    return inner * phi, phi + inner * bell * ((2.0 * math.pi) ** -0.5)


def scalar_call(kernel, name, micros, scalars, operands, out_shapes, scratch, specs=None, outs=None):
    whole = pl.BlockSpec(memory_space=pltpu.VMEM)
    specs = specs or {}
    outs = outs or {}
    return pl.pallas_call(
        kernel,
        grid_spec=pltpu.PrefetchScalarGridSpec(
            num_scalar_prefetch=len(scalars),
            grid=(1,),
            in_specs=[specs.get(at, whole) for at in range(len(operands))],
            out_specs=[outs.get(at, whole) for at in range(len(out_shapes))],
            scratch_shapes=scratch,
        ),
        out_shape=[jax.ShapeDtypeStruct(*item) for item in out_shapes],
        compiler_params=pltpu.CompilerParams(vmem_limit_bytes=VMEM_BYTES),
        cost_estimate=pl.CostEstimate(
            flops=int(micros * FLOPS_A_MICRO), bytes_accessed=0, transcendentals=0
        ),
        name=name,
    )(*scalars, *operands)


def head_of(index):
    return slice(index * HEAD, (index + 1) * HEAD)


def lanes_of(index):
    return slice(index * BLOCK, (index + 1) * BLOCK)


def heads_apart(block, count):
    if count == 1:
        return block
    rows = []
    for h in range(count):
        parts = [jnp.zeros((HEAD, BLOCK), block.dtype)] * count
        parts[h] = block[head_of(h)]
        rows.append(jnp.concatenate(parts, 1))
    return jnp.concatenate(rows, 0)


def same_pair(code_columns, code_row):
    columns = jnp.concatenate([code_columns] * (code_row.shape[1] // code_columns.shape[1]), 1)
    return columns == code_row


def attend_kernel(count, devices, low_ref, high_ref, me_ref, *refs):
    tokens, refs = refs[: 2 * devices], refs[2 * devices :]
    (matrix_ref, bias_ref, pk_ref, pv_ref, columns_ref, row_ref), refs = refs[:6], refs[6:]
    contexts, refs = refs[:devices], refs[devices:]
    turned_ref, total_ref, q_ref, k_ref, v_ref, q_turned, v_turned = refs
    me = me_ref[0]
    width = count * HEAD
    half = tokens[0].shape[0]
    own_rows = 2 * half
    blocks = q_ref.shape[0] // BLOCK
    groups = total_ref.shape[0]
    group_lanes = count // groups * BLOCK
    for at, token_ref in enumerate(tokens):
        device = me ^ (at // 2)
        place = pl.ds(pl.multiple_of(device * own_rows + (at % 2) * half, half), half)
        projected = dot(token_ref[...], matrix_ref[...]) + bias_ref[...]
        queries = projected[:, :width] * (SCALE * LOG2_E)
        q_ref[place, :] = queries.astype(jnp.bfloat16)
        k_ref[place, :] = projected[:, width : 2 * width].astype(jnp.bfloat16)
        v_ref[place, :] = projected[:, 2 * width :].astype(jnp.bfloat16)
    q_turned[...] = q_ref[...].T
    v_turned[...] = v_ref[...].T
    prefix_turned = pv_ref[...].T

    def query_step(i, carry):
        at = pl.ds(pl.multiple_of(i * BLOCK, BLOCK), BLOCK)
        code_row = row_ref[:, at]
        rows = heads_apart(q_turned[:, at], count)

        def weigh(values, weights):
            low_weights = weights.astype(jnp.bfloat16)
            return jnp.concatenate(
                [dot(values[head_of(h)], low_weights[:, lanes_of(h)]) for h in range(count)], 1
            )

        scores = dot(pk_ref[...], rows)
        top = jnp.max(scores, 0, keepdims=True)
        weights = jnp.exp2(scores - top)
        total = jnp.sum(weights, 0, keepdims=True)
        summed = weigh(prefix_turned, weights)

        def key_step(place, state):
            top, total, summed = state
            seen = same_pair(columns_ref[place, :], code_row)
            seen = jnp.concatenate([seen] * count, 1)
            scores = jnp.where(seen, dot(k_ref[place, :], rows), -jnp.inf)
            new_top = jnp.maximum(top, jnp.max(scores, 0, keepdims=True))
            factor = jnp.exp2(top - new_top)
            weights = jnp.exp2(scores - new_top)
            total = total * factor + jnp.sum(weights, 0, keepdims=True)
            summed = summed * factor + weigh(v_turned[:, place], weights)
            return new_top, total, summed

        low, high = low_ref[i], high_ref[i]
        twos = (high - low) // 2

        def two_blocks(j, state):
            start = pl.multiple_of((low + 2 * j) * BLOCK, BLOCK)
            return key_step(pl.ds(start, 2 * BLOCK), state)

        def one_block(j, state):
            return key_step(pl.ds(pl.multiple_of(j * BLOCK, BLOCK), BLOCK), state)

        state = lax.fori_loop(0, twos, two_blocks, (top, total, summed))
        top, total, summed = lax.fori_loop(low + 2 * twos, high, one_block, state)
        logs = top + jnp.log2(total)
        group_place = pl.ds(pl.multiple_of(i * group_lanes, group_lanes), group_lanes)
        for group in range(groups):
            lanes = slice(group * group_lanes, (group + 1) * group_lanes)
            total_ref[group, :, group_place] = logs[:, lanes]
        summed = summed / total
        turned = jnp.concatenate([summed[:, lanes_of(h)] for h in range(count)], 0)
        turned_ref[:, at] = turned
        context = turned.T.astype(jnp.bfloat16)
        share = min(BLOCK, own_rows)
        for part in range(BLOCK // share):
            first = i * BLOCK + part * share
            device, start = first // own_rows, first % own_rows
            for step, context_ref in enumerate(contexts):

                @pl.when(device ^ me == step)
                def _(context_ref=context_ref, start=start, part=part):
                    inside = pl.ds(pl.multiple_of(start, share), share)
                    context_ref[inside, :] = context[part * share : (part + 1) * share]

        return carry

    lax.fori_loop(0, blocks, query_step, 0)


def groups_of(width):
    return max(width // (2 * HEAD), 1)


def attend(low, high, me, tokens, matrix, bias, prefix_k, prefix_v, columns, row):
    devices = len(tokens) // 2
    rows = row.shape[1]
    width = prefix_k.shape[1]
    count = width // HEAD
    groups = groups_of(width)
    own_rows = rows // devices
    results = scalar_call(
        functools.partial(attend_kernel, count, devices),
        "attend",
        40,
        (low, high, me),
        (*tokens, matrix, bias, prefix_k, prefix_v, columns, row),
        [((own_rows, width), jnp.bfloat16)] * devices
        + [
            ((width, rows), jnp.float32),
            ((groups, 1, count // groups * rows), jnp.float32),
        ]
        + [((rows, width), jnp.bfloat16)] * 3,
        [pltpu.VMEM((width, rows), jnp.bfloat16)] * 2,
    )
    return results[:devices], results[devices:]


def attend_back_kernel(count, devices, low_ref, high_ref, me_ref, *refs):
    pieces, refs = refs[:devices], refs[devices:]
    (q_ref, k_ref, v_ref, pk_ref, pv_ref, turned_ref, total_ref, columns_ref, row_ref), refs = (
        refs[:9],
        refs[9:],
    )
    results, refs = refs[:devices], refs[devices:]
    prefix_ref, refs = refs[0], refs[1:]
    (
        g_ref,
        grads_ref,
        q_turned,
        g_turned,
        q_alone,
        g_alone,
        k_turned,
        q_sum,
        delta_ref,
        k_sum,
        v_sum,
        pk_sum,
        pv_sum,
    ) = refs
    me = me_ref[0]
    width = count * HEAD
    blocks = q_ref.shape[0] // BLOCK
    own_rows = pieces[0].shape[0]

    def rows_of(step):
        return pl.ds(pl.multiple_of((me ^ step) * own_rows, own_rows), own_rows)

    for step, piece_ref in enumerate(pieces):
        g_ref[rows_of(step), :] = piece_ref[...]
    k_turned[...] = k_ref[...].T
    prefix_turned = pk_ref[...].T
    q_sum[...] = jnp.zeros_like(q_sum)
    pk_sum[...] = jnp.zeros_like(pk_sum)
    pv_sum[...] = jnp.zeros_like(pv_sum)

    def wide(i):
        return pl.ds(pl.multiple_of(i * count * BLOCK, count * BLOCK), count * BLOCK)

    def query_part(i):
        return pl.ds(pl.multiple_of(i * BLOCK, BLOCK), BLOCK)

    def pair_of_blocks(i, keys, values, keys_turned, seen, key_total, value_total):
        at = query_part(i)
        scores = dot(keys, q_turned[:, wide(i)])
        grad_weights = dot(values, g_turned[:, wide(i)])
        weights = jnp.exp2(scores - total_ref[0, :, wide(i)])
        if seen is not None:
            seen = jnp.concatenate([same_pair(seen, row_ref[:, at])] * count, 1)
            weights = jnp.where(seen, weights, 0.0)
        grad_scores = weights * (grad_weights - delta_ref[:, wide(i)])
        grad_scores = grad_scores.astype(jnp.bfloat16)
        value_total[...] += dot(weights.astype(jnp.bfloat16), g_alone[wide(i), :])
        key_total[...] += dot(grad_scores, q_alone[wide(i), :])
        for h in range(count):
            q_sum[head_of(h), at] += dot(keys_turned[head_of(h)], grad_scores[:, lanes_of(h)])

    def prepare(i, carry):
        at = query_part(i)
        q_block = q_ref[at, :].T
        g_block = g_ref[at, :].T
        delta = g_block.astype(jnp.float32) * turned_ref[:, at]
        delta_ref[:, wide(i)] = jnp.concatenate(
            [jnp.sum(delta[head_of(h)], 0, keepdims=True) for h in range(count)], 1
        )
        q_apart, g_apart = heads_apart(q_block, count), heads_apart(g_block, count)
        q_turned[:, wide(i)] = q_apart
        g_turned[:, wide(i)] = g_apart
        q_alone[wide(i), :] = q_apart.T
        g_alone[wide(i), :] = g_apart.T
        pair_of_blocks(i, pk_ref[...], pv_ref[...], prefix_turned, None, pk_sum, pv_sum)
        return carry

    lax.fori_loop(0, blocks, prepare, 0)
    prefix_ref[0] = pk_sum[...] * LN_2
    prefix_ref[1] = pv_sum[...]

    def key_step(j, carry):
        place = pl.ds(pl.multiple_of(j * 2 * BLOCK, 2 * BLOCK), 2 * BLOCK)
        k_sum[...] = jnp.zeros_like(k_sum)
        v_sum[...] = jnp.zeros_like(v_sum)
        keys = k_ref[place, :]
        values = v_ref[place, :]
        keys_turned = k_turned[:, place]
        seen = columns_ref[place, :]

        def query_step(i, carry):
            pair_of_blocks(i, keys, values, keys_turned, seen, k_sum, v_sum)
            return carry

        lax.fori_loop(low_ref[2 * j], high_ref[2 * j + 1], query_step, 0)
        grads_ref[place, width : 2 * width] = (k_sum[...] * LN_2).astype(jnp.bfloat16)
        grads_ref[place, 2 * width :] = v_sum[...].astype(jnp.bfloat16)
        return carry

    lax.fori_loop(0, blocks // 2, key_step, 0)
    grads_ref[:, :width] = (q_sum[...] * SCALE).T.astype(jnp.bfloat16)
    for step, result_ref in enumerate(results):
        result_ref[...] = grads_ref[rows_of(step), :]


def attend_back(low, high, me, group, pieces, attended, prefix_k, prefix_v, columns, row):
    devices = len(pieces)
    turned, total, queries, keys, values = attended
    own_rows, all_width = pieces[0].shape
    rows, width = own_rows * devices, all_width // groups_of(all_width)
    prefix = prefix_k.shape[0]
    count = width // HEAD
    specs = {
        at: pl.BlockSpec((few, width), lambda t, *_: (0, group))
        for at, few in enumerate([own_rows] * devices + [rows, rows, rows, prefix, prefix])
    }
    specs[devices + 5] = pl.BlockSpec((width, rows), lambda t, *_: (group, 0))
    specs[devices + 6] = pl.BlockSpec((1, 1, total.shape[2]), lambda t, *_: (group, 0, 0))
    results = scalar_call(
        functools.partial(attend_back_kernel, count, devices),
        "attend_back",
        30,
        (low, high, me),
        (*pieces, queries, keys, values, prefix_k, prefix_v, turned, total, columns, row),
        [((rows // devices, 3 * width), jnp.bfloat16)] * devices
        + [((2, prefix, width), jnp.float32)],
        [
            pltpu.VMEM((rows, width), jnp.bfloat16),
            pltpu.VMEM((rows, 3 * width), jnp.bfloat16),
            pltpu.VMEM((width, count * rows), jnp.bfloat16),
            pltpu.VMEM((width, count * rows), jnp.bfloat16),
            pltpu.VMEM((count * rows, width), jnp.bfloat16),
            pltpu.VMEM((count * rows, width), jnp.bfloat16),
            pltpu.VMEM((width, rows), jnp.bfloat16),
            pltpu.VMEM((width, rows), jnp.float32),
            pltpu.VMEM((1, count * rows), jnp.float32),
            pltpu.VMEM((2 * BLOCK, width), jnp.float32),
            pltpu.VMEM((2 * BLOCK, width), jnp.float32),
            pltpu.VMEM((prefix, width), jnp.float32),
            pltpu.VMEM((prefix, width), jnp.float32),
        ],
        specs=specs,
    )
    return results[:devices], results[devices]


def own_block(me, step, size):
    return pl.ds(pl.multiple_of((me ^ step) * size, size), size)


def mix_kernel(devices, me_ref, *refs):
    contexts, refs = refs[:devices], refs[devices:]
    upper_ref, lower_ref, matrix_ref, bias_ref, normal_ref, inverse_ref = refs
    me = me_ref[0]
    width = contexts[0].shape[1]
    tokens = jnp.concatenate([upper_ref[...], lower_ref[...]], 0)
    total = tokens.astype(jnp.float32) + bias_ref[...]
    for step, context_ref in enumerate(contexts):
        total += dot(context_ref[...], matrix_ref[own_block(me, step, width), :])
    normal_ref[...], inverse_ref[...] = normalize(total)


def mix(me, contexts, upper, lower, matrix, bias):
    rows, width = contexts[0].shape[0], upper.shape[1]
    return scalar_call(
        functools.partial(mix_kernel, len(contexts)),
        "mix",
        5,
        (me,),
        (*contexts, upper, lower, matrix, bias),
        [((rows, width), jnp.float32), ((rows, 1), jnp.float32)],
        [],
    )


def copy_in(sources, targets, sems):
    copies = [
        pltpu.make_async_copy(source, target, sems.at[at])
        for at, (source, target) in enumerate(zip(sources, targets, strict=True))
    ]
    for item in copies:
        item.start()
    return copies


def feed_kernel(parts, pieces, me_ref, core_ref, *refs):
    in_refs, back_refs, refs = refs[:parts], refs[parts : 2 * parts], refs[2 * parts :]
    (normal_ref, gain_one, shift_one, bias_in, bias_back, gain_two, shift_two), refs = (
        refs[:7],
        refs[7:],
    )
    outputs, refs = refs[:pieces], refs[pieces:]
    slope_ref, normal_two, inverse_two, held, total, in_held, back_held, slope_held = refs[:8]
    in_sems, back_sems, slope_sems = refs[8:]
    hidden = in_held.shape[2]
    in_copies = copy_in(in_refs, [in_held.at[t] for t in range(parts)], in_sems)
    back_copies = copy_in(back_refs, [back_held.at[t] for t in range(parts)], back_sems)
    normed = normal_ref[...] * gain_one[...] + shift_one[...]
    held[...] = normed.astype(jnp.bfloat16)
    total[...] = normed + bias_back[...]

    def inner_of(t):
        in_copies[t].wait()
        back_copies[t].wait()
        bias = bias_in[(t % 2) ^ core_ref[0], me_ref[0] ^ (t // 2)]
        return dot(held[...], in_held[t]) + bias

    slopes = []
    following = inner_of(0)
    for t in range(parts):
        inner = following
        if t + 1 < parts:
            following = inner_of(t + 1)
        activated, slope = gelu_pair(inner)
        slope_held[t] = slope.astype(jnp.bfloat16)
        target = slope_ref.at[:, t * hidden : (t + 1) * hidden]
        slopes.append(pltpu.make_async_copy(slope_held.at[t], target, slope_sems.at[t]))
        slopes[-1].start()
        total[...] += dot(activated.astype(jnp.bfloat16), back_held[t])
    normal, inverse = normalize(total[...])
    normal_two[...] = normal
    inverse_two[...] = inverse
    result = (normal * gain_two[...] + shift_two[...]).astype(jnp.bfloat16)
    size = result.shape[0] // pieces
    for at, output_ref in enumerate(outputs):
        output_ref[...] = result[at * size : (at + 1) * size]
    for item in slopes:
        item.wait()


def feed(me, core, ins, backs, normal, gain_one, shift_one, bias_in, bias_back, gain_two, shift_two, pieces):
    parts = len(ins)
    rows, width = normal.shape
    hidden = ins[0].shape[1]
    anywhere = pl.BlockSpec(memory_space=pl.ANY)
    results = scalar_call(
        functools.partial(feed_kernel, parts, pieces),
        "feed",
        22,
        (me, core),
        (*ins, *backs, normal, gain_one, shift_one, bias_in, bias_back, gain_two, shift_two),
        [((rows // pieces, width), jnp.bfloat16)] * pieces
        + [
            ((rows, parts * hidden), jnp.bfloat16),
            ((rows, width), jnp.float32),
            ((rows, 1), jnp.float32),
        ],
        [
            pltpu.VMEM((rows, width), jnp.bfloat16),
            pltpu.VMEM((rows, width), jnp.float32),
            pltpu.VMEM((parts, width, hidden), jnp.bfloat16),
            pltpu.VMEM((parts, hidden, width), jnp.bfloat16),
            pltpu.VMEM((parts, rows, hidden), jnp.bfloat16),
            pltpu.SemaphoreType.DMA((parts,)),
            pltpu.SemaphoreType.DMA((parts,)),
            pltpu.SemaphoreType.DMA((parts,)),
        ],
        specs={at: anywhere for at in range(2 * parts)},
        outs={pieces: anywhere},
    )
    return results[:pieces], results[pieces:]


def feed_back_kernel(parts, devices, me_ref, *refs):
    in_refs, back_refs, refs = refs[:parts], refs[parts : 2 * parts], refs[2 * parts :]
    (
        slope_ref,
        normal_one,
        matrix_ref,
        gradient_ref,
        normal_two,
        inverse_two,
        gain_two,
        inverse_one,
        gain_one,
    ), refs = refs[:9], refs[9:]
    grad_one_ref, refs = refs[0], refs[1:]
    results, refs = refs[:-11], refs[-11:]
    held, total, in_held, back_held, slope_held, normal_held, matrix_held = refs[:7]
    in_sems, back_sems, slope_sems, late_sems = refs[7:]
    hidden = in_held.shape[2]
    back_copies = copy_in(back_refs, [back_held.at[t] for t in range(parts)], back_sems)
    slope_copies = copy_in(
        [slope_ref.at[:, t * hidden : (t + 1) * hidden] for t in range(parts)],
        [slope_held.at[t] for t in range(parts)],
        slope_sems,
    )
    in_copies = copy_in(in_refs, [in_held.at[t] for t in range(parts)], in_sems)
    late_copies = copy_in([normal_one, matrix_ref], [normal_held, matrix_held], late_sems)
    gradient = gradient_ref[...].astype(jnp.float32)
    grad_two = normalize_back(gradient, normal_two[...], inverse_two[...], gain_two[...])
    held[...] = grad_two.astype(jnp.bfloat16)
    total[...] = grad_two

    def inner_of(t):
        back_copies[t].wait()
        slope_copies[t].wait()
        in_copies[t].wait()
        return back_dot(held[...], back_held[t])

    following = inner_of(0)
    for t in range(parts):
        inner = following
        if t + 1 < parts:
            following = inner_of(t + 1)
        grad_inner = (inner * slope_held[t].astype(jnp.float32)).astype(jnp.bfloat16)
        total[...] += back_dot(grad_inner, in_held[t])
    for item in late_copies:
        item.wait()
    grad_one = normalize_back(total[...], normal_held[...], inverse_one[...], gain_one[...])
    grad_one_ref[...] = grad_one
    rounded = grad_one.astype(jnp.bfloat16)
    size = results[0].shape[1]
    for step, result_ref in enumerate(results):
        product = back_dot(rounded, matrix_held[own_block(me_ref[0], step, size), :])
        result_ref[...] = product.astype(jnp.bfloat16)


def feed_back(me, devices, ins, backs, gradient, slope, norms, gain_two, gain_one, matrix):
    normal_one, inverse_one, normal_two, inverse_two = norms
    parts = len(ins)
    rows, width = gradient.shape
    hidden = ins[0].shape[1]
    anywhere = pl.BlockSpec(memory_space=pl.ANY)
    results = scalar_call(
        functools.partial(feed_back_kernel, parts, devices),
        "feed_back",
        18,
        (me,),
        (
            *ins,
            *backs,
            slope,
            normal_one,
            matrix,
            gradient,
            normal_two,
            inverse_two,
            gain_two,
            inverse_one,
            gain_one,
        ),
        [((rows, width), jnp.float32)]
        + [((rows, width // devices), jnp.bfloat16)] * devices,
        [
            pltpu.VMEM((rows, width), jnp.bfloat16),
            pltpu.VMEM((rows, width), jnp.float32),
            pltpu.VMEM((parts, width, hidden), jnp.bfloat16),
            pltpu.VMEM((parts, hidden, width), jnp.bfloat16),
            pltpu.VMEM((parts, rows, hidden), jnp.bfloat16),
            pltpu.VMEM(normal_one.shape, normal_one.dtype),
            pltpu.VMEM(matrix.shape, matrix.dtype),
            pltpu.SemaphoreType.DMA((parts,)),
            pltpu.SemaphoreType.DMA((parts,)),
            pltpu.SemaphoreType.DMA((parts,)),
            pltpu.SemaphoreType.DMA((2,)),
        ],
        specs={at: anywhere for at in range(2 * parts + 3)},
    )
    return results[0], results[1:]


def collect_kernel(devices, *refs):
    pieces, (grad_ref, matrix_ref, result_ref) = refs[:devices], refs[devices:]
    total = grad_ref[...]
    width = pieces[0].shape[1]
    for step, piece_ref in enumerate(pieces):
        total += back_dot(piece_ref[...], matrix_ref[:, step * width : (step + 1) * width])
    result_ref[...] = total.astype(result_ref.dtype)


def collect(pieces, grad_one, matrix, dtype):
    return scalar_call(
        functools.partial(collect_kernel, len(pieces)),
        "collect",
        9,
        (),
        (*pieces, grad_one, matrix),
        [(grad_one.shape, dtype)],
        [],
    )[0]


def local(
    dp_count,
    seq_count,
    first_layer_input,
    cotangent,
    lengths,
    w_qkv,
    bias_qkv,
    w_out,
    bias_out,
    w_in,
    bias_in,
    w_back,
    bias_back,
    norm_gain,
    norm_shift,
    prefix_keys,
    prefix_values,
):
    row_count = first_layer_input.shape[1]
    width = first_layer_input.shape[2]
    layer_count = w_qkv.shape[0]
    hidden = w_in.shape[2]
    all_rows = row_count * seq_count
    own_width = width // seq_count
    me = lax.axis_index("seq")
    core = lax.axis_index("dp") % 2
    me_at = me[None].astype(jnp.int32)
    core_at = core[None].astype(jnp.int32)
    bits = [1 << n for n in range(seq_count.bit_length() - 1)]

    def swap(value, step):
        return lax.ppermute(value, "seq", [(i, i ^ step) for i in range(seq_count)])

    def widen(found, order):
        for bit in order:
            found = found | {
                k | bit: swap(item, bit) for k, item in found.items() if k | bit not in found
            }
        return found

    def exchange(value, order):
        found = widen({0: value}, order)
        return [found[k] for k in range(seq_count)]

    def other_core(value):
        return lax.ppermute(value, "dp", [(i, i ^ 1) for i in range(dp_count)])

    def gather(value):
        return lax.all_gather(value, "dp", axis=0, tiled=True)

    def own_columns(values, axis):
        return lax.dynamic_slice_in_dim(values, me * own_width, own_width, axis)

    pair_at = jnp.arange(lengths.shape[1], dtype=jnp.int32)
    ends = jnp.sum(
        jnp.where(pair_at[:, None] <= pair_at[None, :], lengths[0][:, None], 0), 0, dtype=jnp.int32
    )
    starts = ends - lengths[0]
    places = jnp.arange(all_rows, dtype=jnp.int32)
    codes = jnp.sum((places[:, None] >= ends[None, :]).astype(jnp.int32), 1, dtype=jnp.int32)
    columns = jnp.broadcast_to(codes[:, None], (all_rows, 128))
    row = codes[None, :]
    first = jnp.arange(all_rows // BLOCK, dtype=jnp.int32) * BLOCK
    after = first + BLOCK
    low = jnp.max(jnp.where(starts[None, :] <= first[:, None], starts[None, :], 0), 1) // BLOCK
    high = jnp.min(jnp.where(ends[None, :] >= after[:, None], ends[None, :], all_rows), 1)
    high = (high + BLOCK - 1) // BLOCK

    groups = groups_of(own_width)
    half_rows = row_count // 2
    upper, lower = first_layer_input[0, :half_rows], first_layer_input[0, half_rows:]
    first_tokens = exchange(upper, bits), exchange(lower, bits[::-1])

    share = hidden // dp_count // seq_count

    def after(value, *others):
        return lax.optimization_barrier((value, *others))[0]

    def own_qkv(matrix):
        shard = matrix.reshape(-1, 3, seq_count, own_width)
        return lax.dynamic_slice_in_dim(shard, me, 1, 2).reshape(-1, 3 * own_width)

    def all_qkv(matrix):
        shard = matrix.reshape(-1, 3, seq_count, groups, own_width // groups)
        shard = jnp.transpose(shard, (2, 0, 3, 1, 4))
        blocks = [lax.dynamic_slice_in_dim(shard, me ^ step, 1, 0)[0] for step in range(seq_count)]
        return jnp.concatenate([block.reshape(-1, 3 * own_width) for block in blocks], 1)

    def hidden_share(into, back):
        into = into.reshape(-1, dp_count, seq_count, share)
        into = lax.dynamic_slice_in_dim(into, me, 1, 2).reshape(-1, dp_count * share)
        back = lax.dynamic_slice_in_dim(back, me * share, share, 0).reshape(into.shape)
        both = lax.all_gather(jnp.stack([into, back]), "dp")
        into = both[:, 0].reshape(width, dp_count * share)
        back = both[:, 1].reshape(dp_count * share, width)
        return into, back

    def hidden_first(into, back, both):
        half = dp_count * share // 2
        ins, backs = (
            [
                lax.dynamic_slice_in_dim(item, side * half, half, axis)
                for side in (core, 1 - core)
            ]
            for item, axis in ((into, 1), (back, 0))
        )
        in_found, back_found = {0: ins[0]}, {0: backs[0]}
        for bit in bits if both else bits[:1]:
            in_found[bit] = swap(ins[0], bit)
        for bit in bits if both else bits[-1:]:
            back_found[bit] = swap(backs[0], bit)
        return ins[1], backs[1], in_found, back_found

    def hidden_rest(in_other, back_other, in_found, back_found):
        return in_other, back_other, widen(in_found, bits), widen(back_found, bits[::-1])

    def hidden_all(in_other, back_other, in_found, back_found):
        ins, backs = [in_found[0], in_other], [back_found[0], back_other]
        for step in range(1, seq_count):
            ins += [in_found[step], other_core(in_found[step])]
            backs += [back_found[step], other_core(back_found[step])]
        return ins, backs

    def row_of(values):
        return values.astype(jnp.float32)[None, :]

    def over_dp_swap(value, bit):
        return lax.ppermute(value, "dp", [(i, i ^ bit) for i in range(dp_count)])

    saved = []
    tokens = first_tokens
    mat_own = [gather(own_qkv(w_qkv[0]))]
    came = [mat_own[0]] + [found[bit] for found in first_tokens for bit in bits]
    shares = [hidden_share(*after((w_in[0], w_back[0]), came))]
    mat_outs = [gather(after(w_out[0], came))]
    for layer in range(1, layer_count):
        shares.append(hidden_share(*after((w_in[layer], w_back[layer]), came)))
        mat_own.append(gather(own_qkv(after(w_qkv[layer], came))))
        mat_outs.append(gather(after(w_out[layer], came)))
    parts = hidden_first(*shares[0], True)
    for layer in range(layer_count):
        last = layer + 1 == layer_count
        bias_own = own_columns(bias_qkv[layer].reshape(3, width).astype(jnp.float32), 1)
        bias_own = bias_own.reshape(1, 3 * own_width)
        prefix_k = own_columns(prefix_keys[layer], 1)
        prefix_v = own_columns(prefix_values[layer], 1)
        bias_hidden = bias_in[layer].astype(jnp.float32).reshape(2, dp_count // 2, seq_count, share)
        bias_hidden = jnp.transpose(bias_hidden, (0, 2, 1, 3)).reshape(2, seq_count, 1, -1)
        tokens = [item for pair in zip(*tokens, strict=True) for item in pair]
        contexts, attended = attend(
            low, high, me_at, tokens, mat_own[layer], bias_own, prefix_k, prefix_v, columns, row
        )
        if layer:
            parts = hidden_rest(*parts)
            contexts = after(contexts, parts)
        else:
            contexts = after(contexts, parts)
            parts = hidden_rest(*parts)
        contexts = [contexts[0]] + [swap(contexts[k], k) for k in range(1, seq_count)]
        ins, backs = hidden_all(*parts)
        normal_one, inverse_one = mix(
            me_at, contexts, upper, lower, mat_outs[layer], row_of(bias_out[layer])
        )
        if not last:
            parts = hidden_first(*shares[layer + 1], False)
        outputs, (slope, normal_two, inverse_two) = feed(
            me_at,
            core_at,
            ins,
            backs,
            normal_one,
            row_of(norm_gain[layer, 0]),
            row_of(norm_shift[layer, 0]),
            bias_hidden,
            row_of(bias_back[layer]),
            row_of(norm_gain[layer, 1]),
            row_of(norm_shift[layer, 1]),
            1 if last else 2,
        )
        saved.append(
            (
                (attended, prefix_k, prefix_v),
                (normal_one, inverse_one, normal_two, inverse_two),
                (ins, backs, slope, mat_outs[layer]),
            )
        )
        if last:
            hidden_out = outputs[0]
        else:
            upper, lower = after(outputs, parts)
            tokens = exchange(upper, bits), exchange(lower, bits[::-1])
            if not layer:
                mat_qkv = [gather(all_qkv(after(matrix, upper))) for matrix in w_qkv]

    def over_dp(own):
        stride = 1
        while stride < dp_count:
            own = own + over_dp_swap(own, stride)
            stride *= 2
        return own

    gradient = cotangent[0]
    prefix_grads = []
    for layer in reversed(range(layer_count)):
        (attended, prefix_k, prefix_v), norms, (ins, backs, slope, mat_out) = saved[layer]
        grad_one, pieces = feed_back(
            me_at,
            seq_count,
            ins,
            backs,
            gradient,
            slope,
            norms,
            row_of(norm_gain[layer, 1]),
            row_of(norm_gain[layer, 0]),
            mat_out,
        )
        pieces = [pieces[0]] + [swap(pieces[k], k) for k in range(1, seq_count)]
        grads, layer_grads = [], []
        for group in range(groups):
            found, prefix_grad = attend_back(
                low,
                high,
                me_at,
                group,
                pieces,
                attended,
                prefix_k,
                prefix_v,
                columns,
                row,
            )
            layer_grads.append(prefix_grad)
            if grads:
                found = after(found, grads[-1])
            grads.append([found[0]] + [swap(found[k], k) for k in range(1, seq_count)])
        layer_grads = over_dp(jnp.concatenate(layer_grads, 2))
        layer_grads = after(layer_grads, grads[-1])
        prefix_grads.append([layer_grads] + [swap(layer_grads, k) for k in range(1, seq_count)])
        grads = [grads[group][k] for k in range(seq_count) for group in range(groups)]
        gradient = collect(grads, grad_one, mat_qkv[layer], jnp.float32 if layer else jnp.bfloat16)

    found = [jnp.stack(items) for items in zip(*prefix_grads[::-1], strict=True)]
    for bit in bits:
        found = [jnp.where(me & bit, found[k ^ bit], found[k]) for k in range(seq_count)]
    whole = jnp.concatenate(found, 3)
    return (hidden_out[None], gradient[None], whole[:, 0], whole[:, 1])


def solution(mesh):
    in_specs = (
        P("dp", "seq", None),
        P("dp", "seq", None),
        P("dp", None),
        P(None, "dp", None),
        P(),
        P(None, "dp", None),
        P(),
        P(None, "dp", None),
        P(),
        P(None, "dp", None),
        P(),
        P(),
        P(),
        P(),
        P(),
    )
    out_specs = (P("dp", "seq", None), P("dp", "seq", None), P(), P())
    return jax.shard_map(
        functools.partial(local, mesh.shape["dp"], mesh.shape["seq"]),
        mesh=mesh,
        in_specs=in_specs,
        out_specs=out_specs,
        check_vma=False,
    )
```

```python
import functools
import math

import jax
import jax.numpy as jnp
from jax import lax
from jax.experimental import pallas as pl
from jax.experimental.pallas import tpu as pltpu
from jax.sharding import PartitionSpec as P

HEAD = 64

SCALE = 0.125
LOG2_E = math.log2(math.e)
LN_2 = math.log(2.0)
EPS = 1e-05
BLOCK = 256
VMEM_BYTES = 56 * 2**20
FLOPS_A_MICRO = 1.1e9


def dot(left, right):
    return jnp.dot(left, right, preferred_element_type=jnp.float32)


def back_dot(left, right):
    return lax.dot_general(
        left, right, (((1,), (1,)), ((), ())), preferred_element_type=jnp.float32
    )


def normalize(values):
    center = jnp.mean(values, -1, keepdims=True)
    centered = values - center
    spread = jnp.mean(centered * centered, -1, keepdims=True)
    inverse = lax.rsqrt(spread + EPS)
    return centered * inverse, inverse


def normalize_back(gradient, normal, inverse, gain_row):
    scaled = gradient * gain_row
    first = jnp.mean(scaled, -1, keepdims=True)
    second = jnp.mean(scaled * normal, -1, keepdims=True)
    return (scaled - first - normal * second) * inverse


def gelu_pair(inner):
    size = jnp.abs(inner)
    bell = jnp.exp2(inner * inner * (-0.5 * LOG2_E))
    t = 1.0 / (1.0 + (0.3275911 * 0.5**0.5) * size)
    tail = 0.5 * 1.061405429
    for factor in (-1.453152027, 1.421413741, -0.284496736, 0.254829592):
        tail = tail * t + 0.5 * factor
    tail = tail * t * bell
    phi = jnp.where(inner >= 0.0, 1.0 - tail, tail)
    return inner * phi, phi + inner * bell * ((2.0 * math.pi) ** -0.5)


def scalar_call(kernel, name, micros, scalars, operands, out_shapes, scratch, specs=None, outs=None):
    whole = pl.BlockSpec(memory_space=pltpu.VMEM)
    specs = specs or {}
    outs = outs or {}
    return pl.pallas_call(
        kernel,
        grid_spec=pltpu.PrefetchScalarGridSpec(
            num_scalar_prefetch=len(scalars),
            grid=(1,),
            in_specs=[specs.get(at, whole) for at in range(len(operands))],
            out_specs=[outs.get(at, whole) for at in range(len(out_shapes))],
            scratch_shapes=scratch,
        ),
        out_shape=[jax.ShapeDtypeStruct(*item) for item in out_shapes],
        compiler_params=pltpu.CompilerParams(vmem_limit_bytes=VMEM_BYTES),
        cost_estimate=pl.CostEstimate(
            flops=int(micros * FLOPS_A_MICRO), bytes_accessed=0, transcendentals=0
        ),
        name=name,
    )(*scalars, *operands)


def head_of(index):
    return slice(index * HEAD, (index + 1) * HEAD)


def lanes_of(index):
    return slice(index * BLOCK, (index + 1) * BLOCK)


def heads_apart(block, count):
    if count == 1:
        return block
    rows = []
    for h in range(count):
        parts = [jnp.zeros((HEAD, BLOCK), block.dtype)] * count
        parts[h] = block[head_of(h)]
        rows.append(jnp.concatenate(parts, 1))
    return jnp.concatenate(rows, 0)


def same_pair(code_columns, code_row):
    columns = jnp.concatenate([code_columns] * (code_row.shape[1] // code_columns.shape[1]), 1)
    return columns == code_row


def attend_kernel(count, devices, low_ref, high_ref, me_ref, *refs):
    tokens, refs = refs[: 2 * devices], refs[2 * devices :]
    (matrix_ref, bias_ref, pk_ref, pv_ref, columns_ref, row_ref), refs = refs[:6], refs[6:]
    contexts, refs = refs[:devices], refs[devices:]
    turned_ref, total_ref, q_ref, k_ref, v_ref, q_turned, v_turned = refs
    me = me_ref[0]
    width = count * HEAD
    half = tokens[0].shape[0]
    own_rows = 2 * half
    blocks = q_ref.shape[0] // BLOCK
    groups = total_ref.shape[0]
    group_lanes = count // groups * BLOCK
    for at, token_ref in enumerate(tokens):
        device = me ^ (at // 2)
        place = pl.ds(pl.multiple_of(device * own_rows + (at % 2) * half, half), half)
        projected = dot(token_ref[...], matrix_ref[...]) + bias_ref[...]
        queries = projected[:, :width] * (SCALE * LOG2_E)
        q_ref[place, :] = queries.astype(jnp.bfloat16)
        k_ref[place, :] = projected[:, width : 2 * width].astype(jnp.bfloat16)
        v_ref[place, :] = projected[:, 2 * width :].astype(jnp.bfloat16)
    q_turned[...] = q_ref[...].T
    v_turned[...] = v_ref[...].T
    prefix_turned = pv_ref[...].T

    def query_step(i, carry):
        at = pl.ds(pl.multiple_of(i * BLOCK, BLOCK), BLOCK)
        code_row = row_ref[:, at]
        rows = heads_apart(q_turned[:, at], count)

        def weigh(values, weights):
            low_weights = weights.astype(jnp.bfloat16)
            return jnp.concatenate(
                [dot(values[head_of(h)], low_weights[:, lanes_of(h)]) for h in range(count)], 1
            )

        scores = dot(pk_ref[...], rows)
        top = jnp.max(scores, 0, keepdims=True)
        weights = jnp.exp2(scores - top)
        total = jnp.sum(weights, 0, keepdims=True)
        summed = weigh(prefix_turned, weights)

        def key_step(place, state):
            top, total, summed = state
            seen = same_pair(columns_ref[place, :], code_row)
            seen = jnp.concatenate([seen] * count, 1)
            scores = jnp.where(seen, dot(k_ref[place, :], rows), -jnp.inf)
            new_top = jnp.maximum(top, jnp.max(scores, 0, keepdims=True))
            factor = jnp.exp2(top - new_top)
            weights = jnp.exp2(scores - new_top)
            total = total * factor + jnp.sum(weights, 0, keepdims=True)
            summed = summed * factor + weigh(v_turned[:, place], weights)
            return new_top, total, summed

        low, high = low_ref[i], high_ref[i]
        twos = (high - low) // 2

        def two_blocks(j, state):
            start = pl.multiple_of((low + 2 * j) * BLOCK, BLOCK)
            return key_step(pl.ds(start, 2 * BLOCK), state)

        def one_block(j, state):
            return key_step(pl.ds(pl.multiple_of(j * BLOCK, BLOCK), BLOCK), state)

        state = lax.fori_loop(0, twos, two_blocks, (top, total, summed))
        top, total, summed = lax.fori_loop(low + 2 * twos, high, one_block, state)
        logs = top + jnp.log2(total)
        group_place = pl.ds(pl.multiple_of(i * group_lanes, group_lanes), group_lanes)
        for group in range(groups):
            lanes = slice(group * group_lanes, (group + 1) * group_lanes)
            total_ref[group, :, group_place] = logs[:, lanes]
        summed = summed / total
        turned = jnp.concatenate([summed[:, lanes_of(h)] for h in range(count)], 0)
        turned_ref[:, at] = turned
        context = turned.T.astype(jnp.bfloat16)
        share = min(BLOCK, own_rows)
        for part in range(BLOCK // share):
            first = i * BLOCK + part * share
            device, start = first // own_rows, first % own_rows
            for step, context_ref in enumerate(contexts):

                @pl.when(device ^ me == step)
                def _(context_ref=context_ref, start=start, part=part):
                    inside = pl.ds(pl.multiple_of(start, share), share)
                    context_ref[inside, :] = context[part * share : (part + 1) * share]

        return carry

    lax.fori_loop(0, blocks, query_step, 0)


def groups_of(width):
    return max(width // (2 * HEAD), 1)


def attend(low, high, me, tokens, matrix, bias, prefix_k, prefix_v, columns, row):
    devices = len(tokens) // 2
    rows = row.shape[1]
    width = prefix_k.shape[1]
    count = width // HEAD
    groups = groups_of(width)
    own_rows = rows // devices
    results = scalar_call(
        functools.partial(attend_kernel, count, devices),
        "attend",
        40,
        (low, high, me),
        (*tokens, matrix, bias, prefix_k, prefix_v, columns, row),
        [((own_rows, width), jnp.bfloat16)] * devices
        + [
            ((width, rows), jnp.float32),
            ((groups, 1, count // groups * rows), jnp.float32),
        ]
        + [((rows, width), jnp.bfloat16)] * 3,
        [pltpu.VMEM((width, rows), jnp.bfloat16)] * 2,
    )
    return results[:devices], results[devices:]


def attend_back_kernel(count, devices, low_ref, high_ref, me_ref, *refs):
    pieces, refs = refs[:devices], refs[devices:]
    (q_ref, k_ref, v_ref, pk_ref, pv_ref, turned_ref, total_ref, columns_ref, row_ref), refs = (
        refs[:9],
        refs[9:],
    )
    results, refs = refs[:devices], refs[devices:]
    prefix_ref, refs = refs[0], refs[1:]
    (
        g_ref,
        grads_ref,
        q_turned,
        g_turned,
        q_alone,
        g_alone,
        k_turned,
        q_sum,
        delta_ref,
        k_sum,
        v_sum,
        pk_sum,
        pv_sum,
    ) = refs
    me = me_ref[0]
    width = count * HEAD
    blocks = q_ref.shape[0] // BLOCK
    own_rows = pieces[0].shape[0]

    def rows_of(step):
        return pl.ds(pl.multiple_of((me ^ step) * own_rows, own_rows), own_rows)

    for step, piece_ref in enumerate(pieces):
        g_ref[rows_of(step), :] = piece_ref[...]
    k_turned[...] = k_ref[...].T
    prefix_turned = pk_ref[...].T
    q_sum[...] = jnp.zeros_like(q_sum)
    pk_sum[...] = jnp.zeros_like(pk_sum)
    pv_sum[...] = jnp.zeros_like(pv_sum)

    def wide(i):
        return pl.ds(pl.multiple_of(i * count * BLOCK, count * BLOCK), count * BLOCK)

    def query_part(i):
        return pl.ds(pl.multiple_of(i * BLOCK, BLOCK), BLOCK)

    def pair_of_blocks(i, keys, values, keys_turned, seen, key_total, value_total):
        at = query_part(i)
        scores = dot(keys, q_turned[:, wide(i)])
        grad_weights = dot(values, g_turned[:, wide(i)])
        weights = jnp.exp2(scores - total_ref[0, :, wide(i)])
        if seen is not None:
            seen = jnp.concatenate([same_pair(seen, row_ref[:, at])] * count, 1)
            weights = jnp.where(seen, weights, 0.0)
        grad_scores = weights * (grad_weights - delta_ref[:, wide(i)])
        grad_scores = grad_scores.astype(jnp.bfloat16)
        value_total[...] += dot(weights.astype(jnp.bfloat16), g_alone[wide(i), :])
        key_total[...] += dot(grad_scores, q_alone[wide(i), :])
        for h in range(count):
            q_sum[head_of(h), at] += dot(keys_turned[head_of(h)], grad_scores[:, lanes_of(h)])

    lane = lax.broadcasted_iota(jnp.int32, (1, width), 1)

    def prepare(i, carry):
        at = query_part(i)
        q_block = q_ref[at, :].T
        g_block = g_ref[at, :].T
        delta = g_block.astype(jnp.float32) * turned_ref[:, at]
        delta_ref[:, wide(i)] = jnp.concatenate(
            [jnp.sum(delta[head_of(h)], 0, keepdims=True) for h in range(count)], 1
        )
        q_apart, g_apart = heads_apart(q_block, count), heads_apart(g_block, count)
        q_turned[:, wide(i)] = q_apart
        g_turned[:, wide(i)] = g_apart
        for h in range(count):
            own = (lane // HEAD == h).astype(jnp.bfloat16)
            alone = pl.ds(pl.multiple_of((i * count + h) * BLOCK, BLOCK), BLOCK)
            q_alone[alone, :] = q_ref[at, :] * own
            g_alone[alone, :] = g_ref[at, :] * own
        pair_of_blocks(i, pk_ref[...], pv_ref[...], prefix_turned, None, pk_sum, pv_sum)
        return carry

    lax.fori_loop(0, blocks, prepare, 0)
    prefix_ref[0] = pk_sum[...] * LN_2
    prefix_ref[1] = pv_sum[...]

    def key_step(j, carry):
        place = pl.ds(pl.multiple_of(j * 2 * BLOCK, 2 * BLOCK), 2 * BLOCK)
        k_sum[...] = jnp.zeros_like(k_sum)
        v_sum[...] = jnp.zeros_like(v_sum)
        keys = k_ref[place, :]
        values = v_ref[place, :]
        keys_turned = k_turned[:, place]
        seen = columns_ref[place, :]

        def query_step(i, carry):
            pair_of_blocks(i, keys, values, keys_turned, seen, k_sum, v_sum)
            return carry

        lax.fori_loop(low_ref[2 * j], high_ref[2 * j + 1], query_step, 0)
        grads_ref[place, width : 2 * width] = (k_sum[...] * LN_2).astype(jnp.bfloat16)
        grads_ref[place, 2 * width :] = v_sum[...].astype(jnp.bfloat16)
        return carry

    lax.fori_loop(0, blocks // 2, key_step, 0)
    grads_ref[:, :width] = (q_sum[...] * SCALE).T.astype(jnp.bfloat16)
    for step, result_ref in enumerate(results):
        result_ref[...] = grads_ref[rows_of(step), :]


def attend_back(low, high, me, group, pieces, attended, prefix_k, prefix_v, columns, row):
    devices = len(pieces)
    turned, total, queries, keys, values = attended
    own_rows, all_width = pieces[0].shape
    rows, width = own_rows * devices, all_width // groups_of(all_width)
    prefix = prefix_k.shape[0]
    count = width // HEAD
    specs = {
        at: pl.BlockSpec((few, width), lambda t, *_: (0, group))
        for at, few in enumerate([own_rows] * devices + [rows, rows, rows, prefix, prefix])
    }
    specs[devices + 5] = pl.BlockSpec((width, rows), lambda t, *_: (group, 0))
    specs[devices + 6] = pl.BlockSpec((1, 1, total.shape[2]), lambda t, *_: (group, 0, 0))
    results = scalar_call(
        functools.partial(attend_back_kernel, count, devices),
        "attend_back",
        30,
        (low, high, me),
        (*pieces, queries, keys, values, prefix_k, prefix_v, turned, total, columns, row),
        [((rows // devices, 3 * width), jnp.bfloat16)] * devices
        + [((2, prefix, width), jnp.float32)],
        [
            pltpu.VMEM((rows, width), jnp.bfloat16),
            pltpu.VMEM((rows, 3 * width), jnp.bfloat16),
            pltpu.VMEM((width, count * rows), jnp.bfloat16),
            pltpu.VMEM((width, count * rows), jnp.bfloat16),
            pltpu.VMEM((count * rows, width), jnp.bfloat16),
            pltpu.VMEM((count * rows, width), jnp.bfloat16),
            pltpu.VMEM((width, rows), jnp.bfloat16),
            pltpu.VMEM((width, rows), jnp.float32),
            pltpu.VMEM((1, count * rows), jnp.float32),
            pltpu.VMEM((2 * BLOCK, width), jnp.float32),
            pltpu.VMEM((2 * BLOCK, width), jnp.float32),
            pltpu.VMEM((prefix, width), jnp.float32),
            pltpu.VMEM((prefix, width), jnp.float32),
        ],
        specs=specs,
    )
    return results[:devices], results[devices]


def own_block(me, step, size):
    return pl.ds(pl.multiple_of((me ^ step) * size, size), size)


def mix_kernel(devices, me_ref, *refs):
    contexts, refs = refs[:devices], refs[devices:]
    upper_ref, lower_ref, matrix_ref, bias_ref, normal_ref, inverse_ref = refs
    me = me_ref[0]
    width = contexts[0].shape[1]
    tokens = jnp.concatenate([upper_ref[...], lower_ref[...]], 0)
    total = tokens.astype(jnp.float32) + bias_ref[...]
    for step, context_ref in enumerate(contexts):
        total += dot(context_ref[...], matrix_ref[own_block(me, step, width), :])
    normal_ref[...], inverse_ref[...] = normalize(total)


def mix(me, contexts, upper, lower, matrix, bias):
    rows, width = contexts[0].shape[0], upper.shape[1]
    return scalar_call(
        functools.partial(mix_kernel, len(contexts)),
        "mix",
        5,
        (me,),
        (*contexts, upper, lower, matrix, bias),
        [((rows, width), jnp.float32), ((rows, 1), jnp.float32)],
        [],
    )


def copy_in(sources, targets, sems):
    copies = [
        pltpu.make_async_copy(source, target, sems.at[at])
        for at, (source, target) in enumerate(zip(sources, targets, strict=True))
    ]
    for item in copies:
        item.start()
    return copies


def feed_kernel(parts, pieces, me_ref, core_ref, *refs):
    in_refs, back_refs, refs = refs[:parts], refs[parts : 2 * parts], refs[2 * parts :]
    (normal_ref, gain_one, shift_one, bias_in, bias_back, gain_two, shift_two), refs = (
        refs[:7],
        refs[7:],
    )
    outputs, refs = refs[:pieces], refs[pieces:]
    slope_ref, normal_two, inverse_two, held, total, in_held, back_held, slope_held = refs[:8]
    in_sems, back_sems, slope_sems = refs[8:]
    hidden = in_held.shape[2]
    in_copies = copy_in(in_refs, [in_held.at[t] for t in range(parts)], in_sems)
    back_copies = copy_in(back_refs, [back_held.at[t] for t in range(parts)], back_sems)
    normed = normal_ref[...] * gain_one[...] + shift_one[...]
    held[...] = normed.astype(jnp.bfloat16)
    total[...] = normed + bias_back[...]

    def inner_of(t):
        in_copies[t].wait()
        back_copies[t].wait()
        bias = bias_in[(t % 2) ^ core_ref[0], me_ref[0] ^ (t // 2)]
        return dot(held[...], in_held[t]) + bias

    slopes = []
    following = inner_of(0)
    for t in range(parts):
        inner = following
        if t + 1 < parts:
            following = inner_of(t + 1)
        activated, slope = gelu_pair(inner)
        slope_held[t] = slope.astype(jnp.bfloat16)
        target = slope_ref.at[:, t * hidden : (t + 1) * hidden]
        slopes.append(pltpu.make_async_copy(slope_held.at[t], target, slope_sems.at[t]))
        slopes[-1].start()
        total[...] += dot(activated.astype(jnp.bfloat16), back_held[t])
    normal, inverse = normalize(total[...])
    normal_two[...] = normal
    inverse_two[...] = inverse
    result = (normal * gain_two[...] + shift_two[...]).astype(jnp.bfloat16)
    size = result.shape[0] // pieces
    for at, output_ref in enumerate(outputs):
        output_ref[...] = result[at * size : (at + 1) * size]
    for item in slopes:
        item.wait()


def feed(me, core, ins, backs, normal, gain_one, shift_one, bias_in, bias_back, gain_two, shift_two, pieces):
    parts = len(ins)
    rows, width = normal.shape
    hidden = ins[0].shape[1]
    anywhere = pl.BlockSpec(memory_space=pl.ANY)
    results = scalar_call(
        functools.partial(feed_kernel, parts, pieces),
        "feed",
        22,
        (me, core),
        (*ins, *backs, normal, gain_one, shift_one, bias_in, bias_back, gain_two, shift_two),
        [((rows // pieces, width), jnp.bfloat16)] * pieces
        + [
            ((rows, parts * hidden), jnp.bfloat16),
            ((rows, width), jnp.float32),
            ((rows, 1), jnp.float32),
        ],
        [
            pltpu.VMEM((rows, width), jnp.bfloat16),
            pltpu.VMEM((rows, width), jnp.float32),
            pltpu.VMEM((parts, width, hidden), jnp.bfloat16),
            pltpu.VMEM((parts, hidden, width), jnp.bfloat16),
            pltpu.VMEM((parts, rows, hidden), jnp.bfloat16),
            pltpu.SemaphoreType.DMA((parts,)),
            pltpu.SemaphoreType.DMA((parts,)),
            pltpu.SemaphoreType.DMA((parts,)),
        ],
        specs={at: anywhere for at in range(2 * parts)},
        outs={pieces: anywhere},
    )
    return results[:pieces], results[pieces:]


def collect_copies(pieces, matrix_ref, grad_ref, held):
    piece_held, matrix_held, grad_held, piece_sems, matrix_sems, grad_sem = held
    width = pieces[0].shape[1]
    every = range(len(pieces))
    grad_copy = pltpu.make_async_copy(grad_ref, grad_held, grad_sem.at[0])
    piece_copies, matrix_copies = [], []
    for at in every:
        piece_copies += copy_in([pieces[at]], [piece_held.at[at]], piece_sems.at[at : at + 1])
        if matrix_held.shape[0] > at:
            block = matrix_ref
            if matrix_held.shape[0] > 1:
                block = matrix_ref.at[:, at * width : (at + 1) * width]
            matrix_copies += copy_in([block], [matrix_held.at[at]], matrix_sems.at[at : at + 1])
    grad_copy.start()
    return grad_copy, piece_copies, matrix_copies


def collect_held(copies, held):
    grad_copy, piece_copies, matrix_copies = copies
    total = None
    width = held[0].shape[2]
    for at, piece_copy in enumerate(piece_copies):
        piece_copy.wait()
        if at < len(matrix_copies):
            matrix_copies[at].wait()
        if len(matrix_copies) > 1:
            block = held[1][at]
        else:
            block = held[1][0, :, at * width : (at + 1) * width]
        product = back_dot(held[0][at], block)
        total = product if total is None else total + product
    grad_copy.wait()
    return total + held[2][...]


def collect_scratch(pieces, matrix, grad):
    count = len(pieces)
    rows, width = pieces[0].shape
    blocks = 1 if width % 128 else count
    return [
        pltpu.VMEM((count, rows, width), jnp.bfloat16),
        pltpu.VMEM((blocks, matrix.shape[0], matrix.shape[1] // blocks), jnp.bfloat16),
        pltpu.VMEM(grad.shape, grad.dtype),
        pltpu.SemaphoreType.DMA((count,)),
        pltpu.SemaphoreType.DMA((count,)),
        pltpu.SemaphoreType.DMA((1,)),
    ]


def collect_kernel(count, *refs):
    pieces, (matrix_ref, grad_ref, result_ref), held = refs[:count], refs[count : count + 3], refs[count + 3 :]
    copies = collect_copies(pieces, matrix_ref, grad_ref, held)
    result_ref[...] = collect_held(copies, held).astype(result_ref.dtype)


def collect(pieces, matrix, grad):
    return scalar_call(
        functools.partial(collect_kernel, len(pieces)),
        "collect",
        9,
        (),
        (*pieces, matrix, grad),
        [(grad.shape, jnp.bfloat16)],
        collect_scratch(pieces, matrix, grad),
        specs={at: pl.BlockSpec(memory_space=pl.ANY) for at in range(len(pieces) + 2)},
    )[0]


def feed_back_kernel(parts, devices, count, me_ref, *refs):
    in_refs, back_refs, refs = refs[:parts], refs[parts : 2 * parts], refs[2 * parts :]
    (
        slope_ref,
        normal_one,
        matrix_ref,
    ), refs = refs[:3], refs[3:]
    behind, refs = refs[: max(count + 2, 1)], refs[max(count + 2, 1) :]
    (normal_two, inverse_two, gain_two, inverse_one, gain_one), refs = refs[:5], refs[5:]
    grad_one_ref, refs = refs[0], refs[1:]
    results, refs = refs[:devices], refs[devices:]
    held, total, in_held, back_held, slope_held, normal_held, matrix_held = refs[:7]
    in_sems, back_sems, slope_sems, late_sems = refs[7:11]
    hidden = in_held.shape[2]
    if count > 0:
        collected = collect_copies(behind[:count], behind[count], behind[count + 1], refs[11:])
    back_copies = copy_in(back_refs, [back_held.at[t] for t in range(parts)], back_sems)
    slope_copies = copy_in(
        [slope_ref.at[:, t * hidden : (t + 1) * hidden] for t in range(parts)],
        [slope_held.at[t] for t in range(parts)],
        slope_sems,
    )
    in_copies = copy_in(in_refs, [in_held.at[t] for t in range(parts)], in_sems)
    late_copies = copy_in([normal_one, matrix_ref], [normal_held, matrix_held], late_sems)
    if count > 0:
        gradient = collect_held(collected, refs[11:])
    else:
        gradient = behind[0][...].astype(jnp.float32)
    grad_two = normalize_back(gradient, normal_two[...], inverse_two[...], gain_two[...])
    held[...] = grad_two.astype(jnp.bfloat16)
    total[...] = grad_two

    def inner_of(t):
        back_copies[t].wait()
        slope_copies[t].wait()
        in_copies[t].wait()
        return back_dot(held[...], back_held[t])

    following = inner_of(0)
    for t in range(parts):
        inner = following
        if t + 1 < parts:
            following = inner_of(t + 1)
        grad_inner = (inner * slope_held[t].astype(jnp.float32)).astype(jnp.bfloat16)
        total[...] += back_dot(grad_inner, in_held[t])
    for item in late_copies:
        item.wait()
    grad_one = normalize_back(total[...], normal_held[...], inverse_one[...], gain_one[...])
    grad_one_ref[...] = grad_one
    rounded = grad_one.astype(jnp.bfloat16)
    size = results[0].shape[1]
    for step, result_ref in enumerate(results):
        product = back_dot(rounded, matrix_held[own_block(me_ref[0], step, size), :])
        result_ref[...] = product.astype(jnp.bfloat16)


def feed_back(me, devices, ins, backs, behind, slope, norms, gain_two, gain_one, matrix):
    normal_one, inverse_one, normal_two, inverse_two = norms
    parts = len(ins)
    rows, width = normal_one.shape
    count = len(behind) - 2
    hidden = ins[0].shape[1]
    anywhere = pl.BlockSpec(memory_space=pl.ANY)
    results = scalar_call(
        functools.partial(feed_back_kernel, parts, devices, count),
        "feed_back",
        18,
        (me,),
        (
            *ins,
            *backs,
            slope,
            normal_one,
            matrix,
            *behind,
            normal_two,
            inverse_two,
            gain_two,
            inverse_one,
            gain_one,
        ),
        [((rows, width), jnp.float32)]
        + [((rows, width // devices), jnp.bfloat16)] * devices,
        [
            pltpu.VMEM((rows, width), jnp.bfloat16),
            pltpu.VMEM((rows, width), jnp.float32),
            pltpu.VMEM((parts, width, hidden), jnp.bfloat16),
            pltpu.VMEM((parts, hidden, width), jnp.bfloat16),
            pltpu.VMEM((parts, rows, hidden), jnp.bfloat16),
            pltpu.VMEM(normal_one.shape, normal_one.dtype),
            pltpu.VMEM(matrix.shape, matrix.dtype),
            pltpu.SemaphoreType.DMA((parts,)),
            pltpu.SemaphoreType.DMA((parts,)),
            pltpu.SemaphoreType.DMA((parts,)),
            pltpu.SemaphoreType.DMA((2,)),
        ]
        + (collect_scratch(behind[:count], behind[count], behind[count + 1]) if count > 0 else []),
        specs={at: anywhere for at in range(2 * parts + 3 + (count + 2 if count > 0 else 0))},
    )
    return results[0], results[1:]


def local(
    dp_count,
    seq_count,
    first_layer_input,
    cotangent,
    lengths,
    w_qkv,
    bias_qkv,
    w_out,
    bias_out,
    w_in,
    bias_in,
    w_back,
    bias_back,
    norm_gain,
    norm_shift,
    prefix_keys,
    prefix_values,
):
    row_count = first_layer_input.shape[1]
    width = first_layer_input.shape[2]
    layer_count = w_qkv.shape[0]
    hidden = w_in.shape[2]
    all_rows = row_count * seq_count
    own_width = width // seq_count
    me = lax.axis_index("seq")
    core = lax.axis_index("dp") % 2
    me_at = me[None].astype(jnp.int32)
    core_at = core[None].astype(jnp.int32)
    bits = [1 << n for n in range(seq_count.bit_length() - 1)]

    def swap(value, step):
        return lax.ppermute(value, "seq", [(i, i ^ step) for i in range(seq_count)])

    def widen(found, order):
        for bit in order:
            found = found | {
                k | bit: swap(item, bit) for k, item in found.items() if k | bit not in found
            }
        return found

    def exchange(value, order):
        found = widen({0: value}, order)
        return [found[k] for k in range(seq_count)]

    def other_core(value):
        return lax.ppermute(value, "dp", [(i, i ^ 1) for i in range(dp_count)])

    def gather(value):
        return lax.all_gather(value, "dp", axis=0, tiled=True)

    def own_columns(values, axis):
        return lax.dynamic_slice_in_dim(values, me * own_width, own_width, axis)

    pair_at = jnp.arange(lengths.shape[1], dtype=jnp.int32)
    ends = jnp.sum(
        jnp.where(pair_at[:, None] <= pair_at[None, :], lengths[0][:, None], 0), 0, dtype=jnp.int32
    )
    starts = ends - lengths[0]
    places = jnp.arange(all_rows, dtype=jnp.int32)
    codes = jnp.sum((places[:, None] >= ends[None, :]).astype(jnp.int32), 1, dtype=jnp.int32)
    columns = jnp.broadcast_to(codes[:, None], (all_rows, 128))
    row = codes[None, :]
    first = jnp.arange(all_rows // BLOCK, dtype=jnp.int32) * BLOCK
    after = first + BLOCK
    low = jnp.max(jnp.where(starts[None, :] <= first[:, None], starts[None, :], 0), 1) // BLOCK
    high = jnp.min(jnp.where(ends[None, :] >= after[:, None], ends[None, :], all_rows), 1)
    high = (high + BLOCK - 1) // BLOCK

    groups = groups_of(own_width)
    half_rows = row_count // 2
    upper, lower = first_layer_input[0, :half_rows], first_layer_input[0, half_rows:]
    first_tokens = exchange(upper, bits), exchange(lower, bits[::-1])

    share = hidden // dp_count // seq_count

    def after(value, *others):
        return lax.optimization_barrier((value, *others))[0]

    def own_qkv(matrix):
        shard = matrix.reshape(-1, 3, seq_count, own_width)
        return lax.dynamic_slice_in_dim(shard, me, 1, 2).reshape(-1, 3 * own_width)

    def all_qkv(matrix):
        shard = matrix.reshape(-1, 3, seq_count, groups, own_width // groups)
        shard = jnp.transpose(shard, (2, 0, 3, 1, 4))
        blocks = [lax.dynamic_slice_in_dim(shard, me ^ step, 1, 0)[0] for step in range(seq_count)]
        return jnp.concatenate([block.reshape(-1, 3 * own_width) for block in blocks], 1)

    def hidden_share(into, back):
        into = into.reshape(-1, dp_count, seq_count, share)
        into = lax.dynamic_slice_in_dim(into, me, 1, 2).reshape(-1, dp_count * share)
        back = lax.dynamic_slice_in_dim(back, me * share, share, 0).reshape(into.shape)
        both = lax.all_gather(jnp.stack([into, back]), "dp")
        into = both[:, 0].reshape(width, dp_count * share)
        back = both[:, 1].reshape(dp_count * share, width)
        return into, back

    def hidden_first(into, back, both):
        half = dp_count * share // 2
        ins, backs = (
            [
                lax.dynamic_slice_in_dim(item, side * half, half, axis)
                for side in (core, 1 - core)
            ]
            for item, axis in ((into, 1), (back, 0))
        )
        in_found, back_found = {0: ins[0]}, {0: backs[0]}
        for bit in bits if both else bits[:1]:
            in_found[bit] = swap(ins[0], bit)
        for bit in bits if both else bits[-1:]:
            back_found[bit] = swap(backs[0], bit)
        return ins[1], backs[1], in_found, back_found

    def hidden_rest(in_other, back_other, in_found, back_found):
        return in_other, back_other, widen(in_found, bits), widen(back_found, bits[::-1])

    def hidden_all(in_other, back_other, in_found, back_found):
        ins, backs = [in_found[0], in_other], [back_found[0], back_other]
        for step in range(1, seq_count):
            ins += [in_found[step], other_core(in_found[step])]
            backs += [back_found[step], other_core(back_found[step])]
        return ins, backs

    def row_of(values):
        return values.astype(jnp.float32)[None, :]

    def over_dp_swap(value, bit):
        return lax.ppermute(value, "dp", [(i, i ^ bit) for i in range(dp_count)])

    saved = []
    tokens = first_tokens
    shares = [hidden_share(w_in[0], w_back[0])]
    mat_own = [gather(own_qkv(w_qkv[0]))]
    came = [found[bit] for found in first_tokens for bit in bits]
    mat_outs = [gather(after(w_out[0], came))]
    for layer in range(1, layer_count):
        shares.append(hidden_share(*after((w_in[layer], w_back[layer]), tokens)))
        mat_own.append(gather(own_qkv(after(w_qkv[layer], tokens))))
        mat_outs.append(gather(after(w_out[layer], tokens)))
    parts = hidden_first(*shares[0], True)
    for layer in range(layer_count):
        last = layer + 1 == layer_count
        bias_own = own_columns(bias_qkv[layer].reshape(3, width).astype(jnp.float32), 1)
        bias_own = bias_own.reshape(1, 3 * own_width)
        prefix_k = own_columns(prefix_keys[layer], 1)
        prefix_v = own_columns(prefix_values[layer], 1)
        bias_hidden = bias_in[layer].astype(jnp.float32).reshape(2, dp_count // 2, seq_count, share)
        bias_hidden = jnp.transpose(bias_hidden, (0, 2, 1, 3)).reshape(2, seq_count, 1, -1)
        tokens = [item for pair in zip(*tokens, strict=True) for item in pair]
        contexts, attended = attend(
            low, high, me_at, tokens, mat_own[layer], bias_own, prefix_k, prefix_v, columns, row
        )
        if layer:
            parts = hidden_rest(*parts)
            contexts = after(contexts, parts)
        else:
            contexts = after(contexts, parts)
            parts = hidden_rest(*parts)
        contexts = [contexts[0]] + [swap(contexts[k], k) for k in range(1, seq_count)]
        ins, backs = hidden_all(*parts)
        normal_one, inverse_one = mix(
            me_at, contexts, upper, lower, mat_outs[layer], row_of(bias_out[layer])
        )
        if not last:
            parts = hidden_first(*shares[layer + 1], False)
        outputs, (slope, normal_two, inverse_two) = feed(
            me_at,
            core_at,
            ins,
            backs,
            normal_one,
            row_of(norm_gain[layer, 0]),
            row_of(norm_shift[layer, 0]),
            bias_hidden,
            row_of(bias_back[layer]),
            row_of(norm_gain[layer, 1]),
            row_of(norm_shift[layer, 1]),
            1 if last else 2,
        )
        saved.append(
            (
                (attended, prefix_k, prefix_v),
                (normal_one, inverse_one, normal_two, inverse_two),
                (ins, backs, slope, mat_outs[layer]),
            )
        )
        if last:
            hidden_out = outputs[0]
        else:
            upper, lower = after(outputs, parts)
            tokens = exchange(upper, bits), exchange(lower, bits[::-1])
            if not layer:
                mat_qkv = [gather(all_qkv(after(matrix, upper))) for matrix in w_qkv]

    def over_dp(own):
        stride = 1
        while stride < dp_count:
            own = own + over_dp_swap(own, stride)
            stride *= 2
        return own

    behind = [cotangent[0]]
    prefix_grads = []
    for layer in reversed(range(layer_count)):
        (attended, prefix_k, prefix_v), norms, (ins, backs, slope, mat_out) = saved[layer]
        grad_one, pieces = feed_back(
            me_at,
            seq_count,
            ins,
            backs,
            behind,
            slope,
            norms,
            row_of(norm_gain[layer, 1]),
            row_of(norm_gain[layer, 0]),
            mat_out,
        )
        pieces = [pieces[0]] + [swap(pieces[k], k) for k in range(1, seq_count)]
        grads, layer_grads = [], []
        for group in range(groups):
            found, prefix_grad = attend_back(
                low,
                high,
                me_at,
                group,
                pieces,
                attended,
                prefix_k,
                prefix_v,
                columns,
                row,
            )
            layer_grads.append(prefix_grad)
            if grads:
                found = after(found, grads[-1])
            elif prefix_grads:
                found = after(found, prefix_grads[-1])
            grads.append([found[0]] + [swap(found[k], k) for k in range(1, seq_count)])
        layer_grads = over_dp(jnp.concatenate(layer_grads, 2))
        layer_grads = after(layer_grads, grads[-1])
        prefix_grads.append([layer_grads] + [swap(layer_grads, k) for k in range(1, seq_count)])
        grads = [grads[group][k] for k in range(seq_count) for group in range(groups)]
        behind = [*grads, mat_qkv[layer], grad_one]
    gradient = collect(behind[:-2], *behind[-2:])

    found = [jnp.stack(items) for items in zip(*prefix_grads[::-1], strict=True)]
    for bit in bits:
        found = [jnp.where(me & bit, found[k ^ bit], found[k]) for k in range(seq_count)]
    whole = jnp.concatenate(found, 3)
    return (hidden_out[None], gradient[None], whole[:, 0], whole[:, 1])


def solution(mesh):
    in_specs = (
        P("dp", "seq", None),
        P("dp", "seq", None),
        P("dp", None),
        P(None, "dp", None),
        P(),
        P(None, "dp", None),
        P(),
        P(None, "dp", None),
        P(),
        P(None, "dp", None),
        P(),
        P(),
        P(),
        P(),
        P(),
    )
    out_specs = (P("dp", "seq", None), P("dp", "seq", None), P(), P())
    return jax.shard_map(
        functools.partial(local, mesh.shape["dp"], mesh.shape["seq"]),
        mesh=mesh,
        in_specs=in_specs,
        out_specs=out_specs,
        check_vma=False,
    )
```

```python
import functools
import math

import jax
import jax.numpy as jnp
from jax import lax
from jax.experimental import pallas as pl
from jax.experimental.pallas import tpu as pltpu
from jax.sharding import PartitionSpec as P

HEAD = 64

SCALE = 0.125
LOG2_E = math.log2(math.e)
LN_2 = math.log(2.0)
EPS = 1e-05
BLOCK = 256
VMEM_BYTES = 56 * 2**20
FLOPS_A_MICRO = 1.1e9


def dot(left, right):
    return jnp.dot(left, right, preferred_element_type=jnp.float32)


def back_dot(left, right):
    return lax.dot_general(
        left, right, (((1,), (1,)), ((), ())), preferred_element_type=jnp.float32
    )


def normalize(values):
    center = jnp.mean(values, -1, keepdims=True)
    centered = values - center
    spread = jnp.mean(centered * centered, -1, keepdims=True)
    inverse = lax.rsqrt(spread + EPS)
    return centered * inverse, inverse


def normalize_back(gradient, normal, inverse, gain_row):
    scaled = gradient * gain_row
    first = jnp.mean(scaled, -1, keepdims=True)
    second = jnp.mean(scaled * normal, -1, keepdims=True)
    return (scaled - first - normal * second) * inverse


def gelu_pair(inner):
    size = jnp.abs(inner)
    bell = jnp.exp2(inner * inner * (-0.5 * LOG2_E))
    t = 1.0 / (1.0 + (0.3275911 * 0.5**0.5) * size)
    tail = 0.5 * 1.061405429
    for factor in (-1.453152027, 1.421413741, -0.284496736, 0.254829592):
        tail = tail * t + 0.5 * factor
    tail = tail * t * bell
    phi = jnp.where(inner >= 0.0, 1.0 - tail, tail)
    return inner * phi, phi + inner * bell * ((2.0 * math.pi) ** -0.5)


def scalar_call(kernel, name, micros, scalars, operands, out_shapes, scratch, specs=None, outs=None):
    whole = pl.BlockSpec(memory_space=pltpu.VMEM)
    specs = specs or {}
    outs = outs or {}
    return pl.pallas_call(
        kernel,
        grid_spec=pltpu.PrefetchScalarGridSpec(
            num_scalar_prefetch=len(scalars),
            grid=(1,),
            in_specs=[specs.get(at, whole) for at in range(len(operands))],
            out_specs=[outs.get(at, whole) for at in range(len(out_shapes))],
            scratch_shapes=scratch,
        ),
        out_shape=[jax.ShapeDtypeStruct(*item) for item in out_shapes],
        compiler_params=pltpu.CompilerParams(vmem_limit_bytes=VMEM_BYTES),
        cost_estimate=pl.CostEstimate(
            flops=int(micros * FLOPS_A_MICRO), bytes_accessed=0, transcendentals=0
        ),
        name=name,
    )(*scalars, *operands)


def head_of(index):
    return slice(index * HEAD, (index + 1) * HEAD)


def lanes_of(index):
    return slice(index * BLOCK, (index + 1) * BLOCK)


def heads_apart(block, count):
    if count == 1:
        return block
    rows = []
    for h in range(count):
        parts = [jnp.zeros((HEAD, BLOCK), block.dtype)] * count
        parts[h] = block[head_of(h)]
        rows.append(jnp.concatenate(parts, 1))
    return jnp.concatenate(rows, 0)


def same_pair(code_columns, code_row):
    columns = jnp.concatenate([code_columns] * (code_row.shape[1] // code_columns.shape[1]), 1)
    return columns == code_row


def attend_kernel(count, devices, low_ref, high_ref, me_ref, *refs):
    tokens, refs = refs[: 2 * devices], refs[2 * devices :]
    (matrix_ref, bias_ref, pk_ref, pv_ref, columns_ref, row_ref), refs = refs[:6], refs[6:]
    contexts, refs = refs[:devices], refs[devices:]
    turned_ref, total_ref, q_ref, k_ref, v_ref, q_turned, v_turned = refs
    me = me_ref[0]
    width = count * HEAD
    half = tokens[0].shape[0]
    own_rows = 2 * half
    blocks = q_ref.shape[0] // BLOCK
    groups = total_ref.shape[0]
    group_lanes = count // groups * BLOCK
    for at, token_ref in enumerate(tokens):
        device = me ^ (at // 2)
        place = pl.ds(pl.multiple_of(device * own_rows + (at % 2) * half, half), half)
        projected = dot(token_ref[...], matrix_ref[...]) + bias_ref[...]
        queries = projected[:, :width] * (SCALE * LOG2_E)
        q_ref[place, :] = queries.astype(jnp.bfloat16)
        k_ref[place, :] = projected[:, width : 2 * width].astype(jnp.bfloat16)
        v_ref[place, :] = projected[:, 2 * width :].astype(jnp.bfloat16)
    q_turned[...] = q_ref[...].T
    v_turned[...] = v_ref[...].T
    prefix_turned = pv_ref[...].T

    def query_step(i, carry):
        at = pl.ds(pl.multiple_of(i * BLOCK, BLOCK), BLOCK)
        code_row = row_ref[:, at]
        rows = heads_apart(q_turned[:, at], count)

        def weigh(values, weights):
            low_weights = weights.astype(jnp.bfloat16)
            return jnp.concatenate(
                [dot(values[head_of(h)], low_weights[:, lanes_of(h)]) for h in range(count)], 1
            )

        scores = dot(pk_ref[...], rows)
        top = jnp.max(scores, 0, keepdims=True)
        weights = jnp.exp2(scores - top)
        total = jnp.sum(weights, 0, keepdims=True)
        summed = weigh(prefix_turned, weights)

        def key_step(place, state):
            top, total, summed = state
            seen = same_pair(columns_ref[place, :], code_row)
            seen = jnp.concatenate([seen] * count, 1)
            scores = jnp.where(seen, dot(k_ref[place, :], rows), -jnp.inf)
            new_top = jnp.maximum(top, jnp.max(scores, 0, keepdims=True))
            factor = jnp.exp2(top - new_top)
            weights = jnp.exp2(scores - new_top)
            total = total * factor + jnp.sum(weights, 0, keepdims=True)
            summed = summed * factor + weigh(v_turned[:, place], weights)
            return new_top, total, summed

        low, high = low_ref[i], high_ref[i]
        twos = (high - low) // 2

        def two_blocks(j, state):
            start = pl.multiple_of((low + 2 * j) * BLOCK, BLOCK)
            return key_step(pl.ds(start, 2 * BLOCK), state)

        def one_block(j, state):
            return key_step(pl.ds(pl.multiple_of(j * BLOCK, BLOCK), BLOCK), state)

        state = lax.fori_loop(0, twos, two_blocks, (top, total, summed))
        top, total, summed = lax.fori_loop(low + 2 * twos, high, one_block, state)
        logs = top + jnp.log2(total)
        group_place = pl.ds(pl.multiple_of(i * group_lanes, group_lanes), group_lanes)
        for group in range(groups):
            lanes = slice(group * group_lanes, (group + 1) * group_lanes)
            total_ref[group, :, group_place] = logs[:, lanes]
        summed = summed / total
        turned = jnp.concatenate([summed[:, lanes_of(h)] for h in range(count)], 0)
        turned_ref[:, at] = turned
        context = turned.T.astype(jnp.bfloat16)
        share = min(BLOCK, own_rows)
        for part in range(BLOCK // share):
            first = i * BLOCK + part * share
            device, start = first // own_rows, first % own_rows
            for step, context_ref in enumerate(contexts):

                @pl.when(device ^ me == step)
                def _(context_ref=context_ref, start=start, part=part):
                    inside = pl.ds(pl.multiple_of(start, share), share)
                    context_ref[inside, :] = context[part * share : (part + 1) * share]

        return carry

    lax.fori_loop(0, blocks, query_step, 0)


def groups_of(width):
    return max(width // (2 * HEAD), 1)


def attend(low, high, me, tokens, matrix, bias, prefix_k, prefix_v, columns, row):
    devices = len(tokens) // 2
    rows = row.shape[1]
    width = prefix_k.shape[1]
    count = width // HEAD
    groups = groups_of(width)
    own_rows = rows // devices
    results = scalar_call(
        functools.partial(attend_kernel, count, devices),
        "attend",
        40,
        (low, high, me),
        (*tokens, matrix, bias, prefix_k, prefix_v, columns, row),
        [((own_rows, width), jnp.bfloat16)] * devices
        + [
            ((width, rows), jnp.float32),
            ((groups, 1, count // groups * rows), jnp.float32),
        ]
        + [((rows, width), jnp.bfloat16)] * 3,
        [pltpu.VMEM((width, rows), jnp.bfloat16)] * 2,
    )
    return results[:devices], results[devices:]


def attend_back_kernel(count, devices, low_ref, high_ref, me_ref, *refs):
    pieces, refs = refs[:devices], refs[devices:]
    (q_ref, k_ref, v_ref, pk_ref, pv_ref, turned_ref, total_ref, columns_ref, row_ref), refs = (
        refs[:9],
        refs[9:],
    )
    results, refs = refs[:devices], refs[devices:]
    prefix_ref, refs = refs[0], refs[1:]
    (
        g_ref,
        grads_ref,
        q_turned,
        g_turned,
        q_alone,
        g_alone,
        k_turned,
        q_sum,
        delta_ref,
        k_sum,
        v_sum,
        pk_sum,
        pv_sum,
    ) = refs
    me = me_ref[0]
    width = count * HEAD
    blocks = q_ref.shape[0] // BLOCK
    own_rows = pieces[0].shape[0]

    def rows_of(step):
        return pl.ds(pl.multiple_of((me ^ step) * own_rows, own_rows), own_rows)

    for step, piece_ref in enumerate(pieces):
        g_ref[rows_of(step), :] = piece_ref[...]
    k_turned[...] = k_ref[...].T
    prefix_turned = pk_ref[...].T
    q_sum[...] = jnp.zeros_like(q_sum)
    pk_sum[...] = jnp.zeros_like(pk_sum)
    pv_sum[...] = jnp.zeros_like(pv_sum)

    def wide(i):
        return pl.ds(pl.multiple_of(i * count * BLOCK, count * BLOCK), count * BLOCK)

    def query_part(i):
        return pl.ds(pl.multiple_of(i * BLOCK, BLOCK), BLOCK)

    def pair_of_blocks(i, keys, values, keys_turned, seen, key_total, value_total):
        at = query_part(i)
        scores = dot(keys, q_turned[:, wide(i)])
        grad_weights = dot(values, g_turned[:, wide(i)])
        weights = jnp.exp2(scores - total_ref[0, :, wide(i)])
        if seen is not None:
            seen = jnp.concatenate([same_pair(seen, row_ref[:, at])] * count, 1)
            weights = jnp.where(seen, weights, 0.0)
        grad_scores = weights * (grad_weights - delta_ref[:, wide(i)])
        grad_scores = grad_scores.astype(jnp.bfloat16)
        value_total[...] += dot(weights.astype(jnp.bfloat16), g_alone[wide(i), :])
        key_total[...] += dot(grad_scores, q_alone[wide(i), :])
        for h in range(count):
            q_sum[head_of(h), at] += dot(keys_turned[head_of(h)], grad_scores[:, lanes_of(h)])

    lane = lax.broadcasted_iota(jnp.int32, (1, width), 1)

    def prepare(i, carry):
        at = query_part(i)
        q_block = q_ref[at, :].T
        g_block = g_ref[at, :].T
        delta = g_block.astype(jnp.float32) * turned_ref[:, at]
        delta_ref[:, wide(i)] = jnp.concatenate(
            [jnp.sum(delta[head_of(h)], 0, keepdims=True) for h in range(count)], 1
        )
        q_apart, g_apart = heads_apart(q_block, count), heads_apart(g_block, count)
        q_turned[:, wide(i)] = q_apart
        g_turned[:, wide(i)] = g_apart
        for h in range(count):
            own = (lane // HEAD == h).astype(jnp.bfloat16)
            alone = pl.ds(pl.multiple_of((i * count + h) * BLOCK, BLOCK), BLOCK)
            q_alone[alone, :] = q_ref[at, :] * own
            g_alone[alone, :] = g_ref[at, :] * own
        pair_of_blocks(i, pk_ref[...], pv_ref[...], prefix_turned, None, pk_sum, pv_sum)
        return carry

    lax.fori_loop(0, blocks, prepare, 0)
    prefix_ref[0] = pk_sum[...] * LN_2
    prefix_ref[1] = pv_sum[...]

    def key_step(j, carry):
        place = pl.ds(pl.multiple_of(j * 4 * BLOCK, 4 * BLOCK), 4 * BLOCK)
        k_sum[...] = jnp.zeros_like(k_sum)
        v_sum[...] = jnp.zeros_like(v_sum)
        keys = k_ref[place, :]
        values = v_ref[place, :]
        keys_turned = k_turned[:, place]
        seen = columns_ref[place, :]

        def query_step(i, carry):
            pair_of_blocks(i, keys, values, keys_turned, seen, k_sum, v_sum)
            return carry

        lax.fori_loop(low_ref[4 * j], high_ref[4 * j + 3], query_step, 0)
        grads_ref[place, width : 2 * width] = (k_sum[...] * LN_2).astype(jnp.bfloat16)
        grads_ref[place, 2 * width :] = v_sum[...].astype(jnp.bfloat16)
        return carry

    lax.fori_loop(0, blocks // 4, key_step, 0)
    grads_ref[:, :width] = (q_sum[...] * SCALE).T.astype(jnp.bfloat16)
    for step, result_ref in enumerate(results):
        result_ref[...] = grads_ref[rows_of(step), :]


def attend_back(low, high, me, group, pieces, attended, prefix_k, prefix_v, columns, row):
    devices = len(pieces)
    turned, total, queries, keys, values = attended
    own_rows, all_width = pieces[0].shape
    rows, width = own_rows * devices, all_width // groups_of(all_width)
    prefix = prefix_k.shape[0]
    count = width // HEAD
    specs = {
        at: pl.BlockSpec((few, width), lambda t, *_: (0, group))
        for at, few in enumerate([own_rows] * devices + [rows, rows, rows, prefix, prefix])
    }
    specs[devices + 5] = pl.BlockSpec((width, rows), lambda t, *_: (group, 0))
    specs[devices + 6] = pl.BlockSpec((1, 1, total.shape[2]), lambda t, *_: (group, 0, 0))
    results = scalar_call(
        functools.partial(attend_back_kernel, count, devices),
        "attend_back",
        30,
        (low, high, me),
        (*pieces, queries, keys, values, prefix_k, prefix_v, turned, total, columns, row),
        [((rows // devices, 3 * width), jnp.bfloat16)] * devices
        + [((2, prefix, width), jnp.float32)],
        [
            pltpu.VMEM((rows, width), jnp.bfloat16),
            pltpu.VMEM((rows, 3 * width), jnp.bfloat16),
            pltpu.VMEM((width, count * rows), jnp.bfloat16),
            pltpu.VMEM((width, count * rows), jnp.bfloat16),
            pltpu.VMEM((count * rows, width), jnp.bfloat16),
            pltpu.VMEM((count * rows, width), jnp.bfloat16),
            pltpu.VMEM((width, rows), jnp.bfloat16),
            pltpu.VMEM((width, rows), jnp.float32),
            pltpu.VMEM((1, count * rows), jnp.float32),
            pltpu.VMEM((4 * BLOCK, width), jnp.float32),
            pltpu.VMEM((4 * BLOCK, width), jnp.float32),
            pltpu.VMEM((prefix, width), jnp.float32),
            pltpu.VMEM((prefix, width), jnp.float32),
        ],
        specs=specs,
    )
    return results[:devices], results[devices]


def own_block(me, step, size):
    return pl.ds(pl.multiple_of((me ^ step) * size, size), size)


def mix_kernel(devices, me_ref, *refs):
    contexts, refs = refs[:devices], refs[devices:]
    upper_ref, lower_ref, matrix_ref, bias_ref, normal_ref, inverse_ref = refs
    me = me_ref[0]
    width = contexts[0].shape[1]
    tokens = jnp.concatenate([upper_ref[...], lower_ref[...]], 0)
    total = tokens.astype(jnp.float32) + bias_ref[...]
    for step, context_ref in enumerate(contexts):
        total += dot(context_ref[...], matrix_ref[own_block(me, step, width), :])
    normal_ref[...], inverse_ref[...] = normalize(total)


def mix(me, contexts, upper, lower, matrix, bias):
    rows, width = contexts[0].shape[0], upper.shape[1]
    return scalar_call(
        functools.partial(mix_kernel, len(contexts)),
        "mix",
        5,
        (me,),
        (*contexts, upper, lower, matrix, bias),
        [((rows, width), jnp.float32), ((rows, 1), jnp.float32)],
        [],
    )


def copy_in(sources, targets, sems):
    copies = [
        pltpu.make_async_copy(source, target, sems.at[at])
        for at, (source, target) in enumerate(zip(sources, targets, strict=True))
    ]
    for item in copies:
        item.start()
    return copies


def feed_kernel(parts, pieces, me_ref, core_ref, *refs):
    in_refs, back_refs, refs = refs[:parts], refs[parts : 2 * parts], refs[2 * parts :]
    (normal_ref, gain_one, shift_one, bias_in, bias_back, gain_two, shift_two), refs = (
        refs[:7],
        refs[7:],
    )
    outputs, refs = refs[:pieces], refs[pieces:]
    slope_ref, normal_two, inverse_two, held, total, in_held, back_held, slope_held = refs[:8]
    in_sems, back_sems, slope_sems = refs[8:]
    hidden = in_held.shape[2]
    in_copies = copy_in(in_refs, [in_held.at[t] for t in range(parts)], in_sems)
    back_copies = copy_in(back_refs, [back_held.at[t] for t in range(parts)], back_sems)
    normed = normal_ref[...] * gain_one[...] + shift_one[...]
    held[...] = normed.astype(jnp.bfloat16)
    total[...] = normed + bias_back[...]

    def inner_of(t):
        in_copies[t].wait()
        back_copies[t].wait()
        bias = bias_in[(t % 2) ^ core_ref[0], me_ref[0] ^ (t // 2)]
        return dot(held[...], in_held[t]) + bias

    slopes = []
    following = inner_of(0)
    for t in range(parts):
        inner = following
        if t + 1 < parts:
            following = inner_of(t + 1)
        activated, slope = gelu_pair(inner)
        slope_held[t] = slope.astype(jnp.bfloat16)
        target = slope_ref.at[:, t * hidden : (t + 1) * hidden]
        slopes.append(pltpu.make_async_copy(slope_held.at[t], target, slope_sems.at[t]))
        slopes[-1].start()
        total[...] += dot(activated.astype(jnp.bfloat16), back_held[t])
    normal, inverse = normalize(total[...])
    normal_two[...] = normal
    inverse_two[...] = inverse
    result = (normal * gain_two[...] + shift_two[...]).astype(jnp.bfloat16)
    size = result.shape[0] // pieces
    for at, output_ref in enumerate(outputs):
        output_ref[...] = result[at * size : (at + 1) * size]
    for item in slopes:
        item.wait()


def feed(me, core, ins, backs, normal, gain_one, shift_one, bias_in, bias_back, gain_two, shift_two, pieces):
    parts = len(ins)
    rows, width = normal.shape
    hidden = ins[0].shape[1]
    anywhere = pl.BlockSpec(memory_space=pl.ANY)
    results = scalar_call(
        functools.partial(feed_kernel, parts, pieces),
        "feed",
        22,
        (me, core),
        (*ins, *backs, normal, gain_one, shift_one, bias_in, bias_back, gain_two, shift_two),
        [((rows // pieces, width), jnp.bfloat16)] * pieces
        + [
            ((rows, parts * hidden), jnp.bfloat16),
            ((rows, width), jnp.float32),
            ((rows, 1), jnp.float32),
        ],
        [
            pltpu.VMEM((rows, width), jnp.bfloat16),
            pltpu.VMEM((rows, width), jnp.float32),
            pltpu.VMEM((parts, width, hidden), jnp.bfloat16),
            pltpu.VMEM((parts, hidden, width), jnp.bfloat16),
            pltpu.VMEM((parts, rows, hidden), jnp.bfloat16),
            pltpu.SemaphoreType.DMA((parts,)),
            pltpu.SemaphoreType.DMA((parts,)),
            pltpu.SemaphoreType.DMA((parts,)),
        ],
        specs={at: anywhere for at in range(2 * parts)},
        outs={pieces: anywhere},
    )
    return results[:pieces], results[pieces:]


def collect_copies(pieces, matrix_ref, grad_ref, held):
    piece_held, matrix_held, grad_held, piece_sems, matrix_sems, grad_sem = held
    width = pieces[0].shape[1]
    every = range(len(pieces))
    grad_copy = pltpu.make_async_copy(grad_ref, grad_held, grad_sem.at[0])
    piece_copies, matrix_copies = [], []
    for at in every:
        piece_copies += copy_in([pieces[at]], [piece_held.at[at]], piece_sems.at[at : at + 1])
        if matrix_held.shape[0] > at:
            block = matrix_ref
            if matrix_held.shape[0] > 1:
                block = matrix_ref.at[:, at * width : (at + 1) * width]
            matrix_copies += copy_in([block], [matrix_held.at[at]], matrix_sems.at[at : at + 1])
    grad_copy.start()
    return grad_copy, piece_copies, matrix_copies


def collect_held(copies, held):
    grad_copy, piece_copies, matrix_copies = copies
    total = None
    width = held[0].shape[2]
    for at, piece_copy in enumerate(piece_copies):
        piece_copy.wait()
        if at < len(matrix_copies):
            matrix_copies[at].wait()
        if len(matrix_copies) > 1:
            block = held[1][at]
        else:
            block = held[1][0, :, at * width : (at + 1) * width]
        product = back_dot(held[0][at], block)
        total = product if total is None else total + product
    grad_copy.wait()
    return total + held[2][...]


def collect_scratch(pieces, matrix, grad):
    count = len(pieces)
    rows, width = pieces[0].shape
    blocks = 1 if width % 128 else count
    return [
        pltpu.VMEM((count, rows, width), jnp.bfloat16),
        pltpu.VMEM((blocks, matrix.shape[0], matrix.shape[1] // blocks), jnp.bfloat16),
        pltpu.VMEM(grad.shape, grad.dtype),
        pltpu.SemaphoreType.DMA((count,)),
        pltpu.SemaphoreType.DMA((count,)),
        pltpu.SemaphoreType.DMA((1,)),
    ]


def collect_kernel(count, *refs):
    pieces, (matrix_ref, grad_ref, result_ref), held = refs[:count], refs[count : count + 3], refs[count + 3 :]
    copies = collect_copies(pieces, matrix_ref, grad_ref, held)
    result_ref[...] = collect_held(copies, held).astype(result_ref.dtype)


def collect(pieces, matrix, grad):
    return scalar_call(
        functools.partial(collect_kernel, len(pieces)),
        "collect",
        9,
        (),
        (*pieces, matrix, grad),
        [(grad.shape, jnp.bfloat16)],
        collect_scratch(pieces, matrix, grad),
        specs={at: pl.BlockSpec(memory_space=pl.ANY) for at in range(len(pieces) + 2)},
    )[0]


def feed_back_kernel(parts, devices, count, me_ref, *refs):
    in_refs, back_refs, refs = refs[:parts], refs[parts : 2 * parts], refs[2 * parts :]
    (
        slope_ref,
        normal_one,
        matrix_ref,
    ), refs = refs[:3], refs[3:]
    behind, refs = refs[: max(count + 2, 1)], refs[max(count + 2, 1) :]
    (normal_two, inverse_two, gain_two, inverse_one, gain_one), refs = refs[:5], refs[5:]
    grad_one_ref, refs = refs[0], refs[1:]
    results, refs = refs[:devices], refs[devices:]
    held, total, in_held, back_held, slope_held, normal_held, matrix_held = refs[:7]
    in_sems, back_sems, slope_sems, late_sems = refs[7:11]
    hidden = in_held.shape[2]
    if count > 0:
        collected = collect_copies(behind[:count], behind[count], behind[count + 1], refs[11:])
    back_copies = copy_in(back_refs, [back_held.at[t] for t in range(parts)], back_sems)
    slope_copies = copy_in(
        [slope_ref.at[:, t * hidden : (t + 1) * hidden] for t in range(parts)],
        [slope_held.at[t] for t in range(parts)],
        slope_sems,
    )
    in_copies = copy_in(in_refs, [in_held.at[t] for t in range(parts)], in_sems)
    late_copies = copy_in([normal_one, matrix_ref], [normal_held, matrix_held], late_sems)
    if count > 0:
        gradient = collect_held(collected, refs[11:])
    else:
        gradient = behind[0][...].astype(jnp.float32)
    grad_two = normalize_back(gradient, normal_two[...], inverse_two[...], gain_two[...])
    held[...] = grad_two.astype(jnp.bfloat16)
    total[...] = grad_two

    def inner_of(t):
        back_copies[t].wait()
        slope_copies[t].wait()
        in_copies[t].wait()
        return back_dot(held[...], back_held[t])

    following = inner_of(0)
    for t in range(parts):
        inner = following
        if t + 1 < parts:
            following = inner_of(t + 1)
        grad_inner = (inner * slope_held[t].astype(jnp.float32)).astype(jnp.bfloat16)
        total[...] += back_dot(grad_inner, in_held[t])
    for item in late_copies:
        item.wait()
    grad_one = normalize_back(total[...], normal_held[...], inverse_one[...], gain_one[...])
    grad_one_ref[...] = grad_one
    rounded = grad_one.astype(jnp.bfloat16)
    size = results[0].shape[1]
    for step, result_ref in enumerate(results):
        product = back_dot(rounded, matrix_held[own_block(me_ref[0], step, size), :])
        result_ref[...] = product.astype(jnp.bfloat16)


def feed_back(me, devices, ins, backs, behind, slope, norms, gain_two, gain_one, matrix):
    normal_one, inverse_one, normal_two, inverse_two = norms
    parts = len(ins)
    rows, width = normal_one.shape
    count = len(behind) - 2
    hidden = ins[0].shape[1]
    anywhere = pl.BlockSpec(memory_space=pl.ANY)
    results = scalar_call(
        functools.partial(feed_back_kernel, parts, devices, count),
        "feed_back",
        18,
        (me,),
        (
            *ins,
            *backs,
            slope,
            normal_one,
            matrix,
            *behind,
            normal_two,
            inverse_two,
            gain_two,
            inverse_one,
            gain_one,
        ),
        [((rows, width), jnp.float32)]
        + [((rows, width // devices), jnp.bfloat16)] * devices,
        [
            pltpu.VMEM((rows, width), jnp.bfloat16),
            pltpu.VMEM((rows, width), jnp.float32),
            pltpu.VMEM((parts, width, hidden), jnp.bfloat16),
            pltpu.VMEM((parts, hidden, width), jnp.bfloat16),
            pltpu.VMEM((parts, rows, hidden), jnp.bfloat16),
            pltpu.VMEM(normal_one.shape, normal_one.dtype),
            pltpu.VMEM(matrix.shape, matrix.dtype),
            pltpu.SemaphoreType.DMA((parts,)),
            pltpu.SemaphoreType.DMA((parts,)),
            pltpu.SemaphoreType.DMA((parts,)),
            pltpu.SemaphoreType.DMA((2,)),
        ]
        + (collect_scratch(behind[:count], behind[count], behind[count + 1]) if count > 0 else []),
        specs={at: anywhere for at in range(2 * parts + 3 + (count + 2 if count > 0 else 0))},
    )
    return results[0], results[1:]


def local(
    dp_count,
    seq_count,
    first_layer_input,
    cotangent,
    lengths,
    w_qkv,
    bias_qkv,
    w_out,
    bias_out,
    w_in,
    bias_in,
    w_back,
    bias_back,
    norm_gain,
    norm_shift,
    prefix_keys,
    prefix_values,
):
    row_count = first_layer_input.shape[1]
    width = first_layer_input.shape[2]
    layer_count = w_qkv.shape[0]
    hidden = w_in.shape[2]
    all_rows = row_count * seq_count
    own_width = width // seq_count
    me = lax.axis_index("seq")
    core = lax.axis_index("dp") % 2
    me_at = me[None].astype(jnp.int32)
    core_at = core[None].astype(jnp.int32)
    bits = [1 << n for n in range(seq_count.bit_length() - 1)]

    def swap(value, step):
        return lax.ppermute(value, "seq", [(i, i ^ step) for i in range(seq_count)])

    def widen(found, order):
        for bit in order:
            found = found | {
                k | bit: swap(item, bit) for k, item in found.items() if k | bit not in found
            }
        return found

    def exchange(value, order):
        found = widen({0: value}, order)
        return [found[k] for k in range(seq_count)]

    def other_core(value):
        return lax.ppermute(value, "dp", [(i, i ^ 1) for i in range(dp_count)])

    def gather(value):
        return lax.all_gather(value, "dp", axis=0, tiled=True)

    def own_columns(values, axis):
        return lax.dynamic_slice_in_dim(values, me * own_width, own_width, axis)

    pair_at = jnp.arange(lengths.shape[1], dtype=jnp.int32)
    ends = jnp.sum(
        jnp.where(pair_at[:, None] <= pair_at[None, :], lengths[0][:, None], 0), 0, dtype=jnp.int32
    )
    starts = ends - lengths[0]
    places = jnp.arange(all_rows, dtype=jnp.int32)
    codes = jnp.sum((places[:, None] >= ends[None, :]).astype(jnp.int32), 1, dtype=jnp.int32)
    columns = jnp.broadcast_to(codes[:, None], (all_rows, 128))
    row = codes[None, :]
    first = jnp.arange(all_rows // BLOCK, dtype=jnp.int32) * BLOCK
    after = first + BLOCK
    low = jnp.max(jnp.where(starts[None, :] <= first[:, None], starts[None, :], 0), 1) // BLOCK
    high = jnp.min(jnp.where(ends[None, :] >= after[:, None], ends[None, :], all_rows), 1)
    high = (high + BLOCK - 1) // BLOCK

    groups = groups_of(own_width)
    half_rows = row_count // 2
    upper, lower = first_layer_input[0, :half_rows], first_layer_input[0, half_rows:]
    first_tokens = exchange(upper, bits), exchange(lower, bits[::-1])

    share = hidden // dp_count // seq_count

    def after(value, *others):
        return lax.optimization_barrier((value, *others))[0]

    def own_qkv(matrix):
        shard = matrix.reshape(-1, 3, seq_count, own_width)
        return lax.dynamic_slice_in_dim(shard, me, 1, 2).reshape(-1, 3 * own_width)

    def all_qkv(matrix):
        shard = matrix.reshape(-1, 3, seq_count, groups, own_width // groups)
        shard = jnp.transpose(shard, (2, 0, 3, 1, 4))
        blocks = [lax.dynamic_slice_in_dim(shard, me ^ step, 1, 0)[0] for step in range(seq_count)]
        return jnp.concatenate([block.reshape(-1, 3 * own_width) for block in blocks], 1)

    def hidden_share(into, back):
        into = into.reshape(-1, dp_count, seq_count, share)
        into = lax.dynamic_slice_in_dim(into, me, 1, 2).reshape(-1, dp_count * share)
        back = lax.dynamic_slice_in_dim(back, me * share, share, 0).reshape(into.shape)
        both = lax.all_gather(jnp.stack([into, back]), "dp")
        into = both[:, 0].reshape(width, dp_count * share)
        back = both[:, 1].reshape(dp_count * share, width)
        return into, back

    def hidden_first(into, back, both):
        half = dp_count * share // 2
        ins, backs = (
            [
                lax.dynamic_slice_in_dim(item, side * half, half, axis)
                for side in (core, 1 - core)
            ]
            for item, axis in ((into, 1), (back, 0))
        )
        in_found, back_found = {0: ins[0]}, {0: backs[0]}
        for bit in bits if both else bits[:1]:
            in_found[bit] = swap(ins[0], bit)
        for bit in bits if both else bits[-1:]:
            back_found[bit] = swap(backs[0], bit)
        return ins[1], backs[1], in_found, back_found

    def hidden_rest(in_other, back_other, in_found, back_found):
        return in_other, back_other, widen(in_found, bits), widen(back_found, bits[::-1])

    def hidden_all(in_other, back_other, in_found, back_found):
        ins, backs = [in_found[0], in_other], [back_found[0], back_other]
        for step in range(1, seq_count):
            ins += [in_found[step], other_core(in_found[step])]
            backs += [back_found[step], other_core(back_found[step])]
        return ins, backs

    def row_of(values):
        return values.astype(jnp.float32)[None, :]

    def over_dp_swap(value, bit):
        return lax.ppermute(value, "dp", [(i, i ^ bit) for i in range(dp_count)])

    saved = []
    tokens = first_tokens
    shares = [hidden_share(w_in[0], w_back[0])]
    mat_own = [gather(own_qkv(w_qkv[0]))]
    came = [found[bit] for found in first_tokens for bit in bits]
    mat_outs = [gather(after(w_out[0], came))]
    for layer in range(1, layer_count):
        shares.append(hidden_share(*after((w_in[layer], w_back[layer]), tokens)))
        mat_own.append(gather(own_qkv(after(w_qkv[layer], tokens))))
        mat_outs.append(gather(after(w_out[layer], tokens)))
    parts = hidden_first(*shares[0], True)
    for layer in range(layer_count):
        last = layer + 1 == layer_count
        bias_own = own_columns(bias_qkv[layer].reshape(3, width).astype(jnp.float32), 1)
        bias_own = bias_own.reshape(1, 3 * own_width)
        prefix_k = own_columns(prefix_keys[layer], 1)
        prefix_v = own_columns(prefix_values[layer], 1)
        bias_hidden = bias_in[layer].astype(jnp.float32).reshape(2, dp_count // 2, seq_count, share)
        bias_hidden = jnp.transpose(bias_hidden, (0, 2, 1, 3)).reshape(2, seq_count, 1, -1)
        tokens = [item for pair in zip(*tokens, strict=True) for item in pair]
        contexts, attended = attend(
            low, high, me_at, tokens, mat_own[layer], bias_own, prefix_k, prefix_v, columns, row
        )
        if layer:
            parts = hidden_rest(*parts)
            contexts = after(contexts, parts)
        else:
            contexts = after(contexts, parts)
            parts = hidden_rest(*parts)
        contexts = [contexts[0]] + [swap(contexts[k], k) for k in range(1, seq_count)]
        ins, backs = hidden_all(*parts)
        normal_one, inverse_one = mix(
            me_at, contexts, upper, lower, mat_outs[layer], row_of(bias_out[layer])
        )
        if not last:
            parts = hidden_first(*shares[layer + 1], False)
        outputs, (slope, normal_two, inverse_two) = feed(
            me_at,
            core_at,
            ins,
            backs,
            normal_one,
            row_of(norm_gain[layer, 0]),
            row_of(norm_shift[layer, 0]),
            bias_hidden,
            row_of(bias_back[layer]),
            row_of(norm_gain[layer, 1]),
            row_of(norm_shift[layer, 1]),
            1 if last else 2,
        )
        saved.append(
            (
                (attended, prefix_k, prefix_v),
                (normal_one, inverse_one, normal_two, inverse_two),
                (ins, backs, slope, mat_outs[layer]),
            )
        )
        if last:
            hidden_out = outputs[0]
        else:
            upper, lower = after(outputs, parts)
            tokens = exchange(upper, bits), exchange(lower, bits[::-1])
            if not layer:
                mat_qkv = [gather(all_qkv(after(matrix, upper))) for matrix in w_qkv]

    def over_dp(own):
        stride = 1
        while stride < dp_count:
            own = own + over_dp_swap(own, stride)
            stride *= 2
        return own

    behind = [cotangent[0]]
    prefix_grads = []
    for layer in reversed(range(layer_count)):
        (attended, prefix_k, prefix_v), norms, (ins, backs, slope, mat_out) = saved[layer]
        grad_one, pieces = feed_back(
            me_at,
            seq_count,
            ins,
            backs,
            behind,
            slope,
            norms,
            row_of(norm_gain[layer, 1]),
            row_of(norm_gain[layer, 0]),
            mat_out,
        )
        pieces = [pieces[0]] + [swap(pieces[k], k) for k in range(1, seq_count)]
        grads, layer_grads = [], []
        for group in range(groups):
            found, prefix_grad = attend_back(
                low,
                high,
                me_at,
                group,
                pieces,
                attended,
                prefix_k,
                prefix_v,
                columns,
                row,
            )
            layer_grads.append(prefix_grad)
            if grads:
                found = after(found, grads[-1])
            elif prefix_grads:
                found = after(found, prefix_grads[-1])
            grads.append([found[0]] + [swap(found[k], k) for k in range(1, seq_count)])
        layer_grads = over_dp(jnp.concatenate(layer_grads, 2))
        layer_grads = after(layer_grads, grads[-1])
        prefix_grads.append([layer_grads] + [swap(layer_grads, k) for k in range(1, seq_count)])
        grads = [grads[group][k] for k in range(seq_count) for group in range(groups)]
        behind = [*grads, mat_qkv[layer], grad_one]
    gradient = collect(behind[:-2], *behind[-2:])

    found = [jnp.stack(items) for items in zip(*prefix_grads[::-1], strict=True)]
    for bit in bits:
        found = [jnp.where(me & bit, found[k ^ bit], found[k]) for k in range(seq_count)]
    whole = jnp.concatenate(found, 3)
    return (hidden_out[None], gradient[None], whole[:, 0], whole[:, 1])


def solution(mesh):
    in_specs = (
        P("dp", "seq", None),
        P("dp", "seq", None),
        P("dp", None),
        P(None, "dp", None),
        P(),
        P(None, "dp", None),
        P(),
        P(None, "dp", None),
        P(),
        P(None, "dp", None),
        P(),
        P(),
        P(),
        P(),
        P(),
    )
    out_specs = (P("dp", "seq", None), P("dp", "seq", None), P(), P())
    return jax.shard_map(
        functools.partial(local, mesh.shape["dp"], mesh.shape["seq"]),
        mesh=mesh,
        in_specs=in_specs,
        out_specs=out_specs,
        check_vma=False,
    )
```

```python
import functools
import math

import jax
import jax.numpy as jnp
from jax import lax
from jax.experimental import pallas as pl
from jax.experimental.pallas import tpu as pltpu
from jax.sharding import PartitionSpec as P

HEAD = 64

SCALE = 0.125
LOG2_E = math.log2(math.e)
LN_2 = math.log(2.0)
EPS = 1e-05
BLOCK = 256
VMEM_BYTES = 56 * 2**20
FLOPS_A_MICRO = 1.1e9


def dot(left, right):
    return jnp.dot(left, right, preferred_element_type=jnp.float32)


def back_dot(left, right):
    return lax.dot_general(
        left, right, (((1,), (1,)), ((), ())), preferred_element_type=jnp.float32
    )


def normalize(values):
    center = jnp.mean(values, -1, keepdims=True)
    centered = values - center
    spread = jnp.mean(centered * centered, -1, keepdims=True)
    inverse = lax.rsqrt(spread + EPS)
    return centered * inverse, inverse


def normalize_back(gradient, normal, inverse, gain_row):
    scaled = gradient * gain_row
    first = jnp.mean(scaled, -1, keepdims=True)
    second = jnp.mean(scaled * normal, -1, keepdims=True)
    return (scaled - first - normal * second) * inverse


def gelu_pair(inner):
    size = jnp.abs(inner)
    bell = jnp.exp2(inner * inner * (-0.5 * LOG2_E))
    t = 1.0 / (1.0 + (0.3275911 * 0.5**0.5) * size)
    tail = 0.5 * 1.061405429
    for factor in (-1.453152027, 1.421413741, -0.284496736, 0.254829592):
        tail = tail * t + 0.5 * factor
    tail = tail * t * bell
    phi = jnp.where(inner >= 0.0, 1.0 - tail, tail)
    return inner * phi, phi + inner * bell * ((2.0 * math.pi) ** -0.5)


def scalar_call(kernel, name, micros, scalars, operands, out_shapes, scratch, specs=None, outs=None):
    whole = pl.BlockSpec(memory_space=pltpu.VMEM)
    specs = specs or {}
    outs = outs or {}
    return pl.pallas_call(
        kernel,
        grid_spec=pltpu.PrefetchScalarGridSpec(
            num_scalar_prefetch=len(scalars),
            grid=(1,),
            in_specs=[specs.get(at, whole) for at in range(len(operands))],
            out_specs=[outs.get(at, whole) for at in range(len(out_shapes))],
            scratch_shapes=scratch,
        ),
        out_shape=[jax.ShapeDtypeStruct(*item) for item in out_shapes],
        compiler_params=pltpu.CompilerParams(vmem_limit_bytes=VMEM_BYTES),
        cost_estimate=pl.CostEstimate(
            flops=int(micros * FLOPS_A_MICRO), bytes_accessed=0, transcendentals=0
        ),
        name=name,
    )(*scalars, *operands)


def head_of(index):
    return slice(index * HEAD, (index + 1) * HEAD)


def lanes_of(index):
    return slice(index * BLOCK, (index + 1) * BLOCK)


def heads_apart(block, count):
    if count == 1:
        return block
    rows = []
    for h in range(count):
        parts = [jnp.zeros((HEAD, BLOCK), block.dtype)] * count
        parts[h] = block[head_of(h)]
        rows.append(jnp.concatenate(parts, 1))
    return jnp.concatenate(rows, 0)


def same_pair(code_columns, code_row):
    columns = jnp.concatenate([code_columns] * (code_row.shape[1] // code_columns.shape[1]), 1)
    return columns == code_row


def attend_kernel(count, devices, low_ref, high_ref, me_ref, *refs):
    tokens, refs = refs[: 2 * devices], refs[2 * devices :]
    (matrix_ref, bias_ref, pk_ref, pv_ref, columns_ref, row_ref), refs = refs[:6], refs[6:]
    contexts, refs = refs[:devices], refs[devices:]
    turned_ref, total_ref, q_ref, k_ref, v_ref, q_turned, v_turned = refs
    me = me_ref[0]
    width = count * HEAD
    half = tokens[0].shape[0]
    own_rows = 2 * half
    blocks = q_ref.shape[0] // BLOCK
    groups = total_ref.shape[0]
    group_lanes = count // groups * BLOCK
    for at, token_ref in enumerate(tokens):
        device = me ^ (at // 2)
        place = pl.ds(pl.multiple_of(device * own_rows + (at % 2) * half, half), half)
        projected = dot(token_ref[...], matrix_ref[...]) + bias_ref[...]
        queries = projected[:, :width] * (SCALE * LOG2_E)
        q_ref[place, :] = queries.astype(jnp.bfloat16)
        k_ref[place, :] = projected[:, width : 2 * width].astype(jnp.bfloat16)
        v_ref[place, :] = projected[:, 2 * width :].astype(jnp.bfloat16)
    q_turned[...] = q_ref[...].T
    v_turned[...] = v_ref[...].T
    prefix_turned = pv_ref[...].T

    def query_step(i, carry):
        at = pl.ds(pl.multiple_of(i * BLOCK, BLOCK), BLOCK)
        code_row = row_ref[:, at]
        rows = heads_apart(q_turned[:, at], count)

        def weigh(values, weights):
            low_weights = weights.astype(jnp.bfloat16)
            return jnp.concatenate(
                [dot(values[head_of(h)], low_weights[:, lanes_of(h)]) for h in range(count)], 1
            )

        scores = dot(pk_ref[...], rows)
        top = jnp.max(scores, 0, keepdims=True)
        weights = jnp.exp2(scores - top)
        total = jnp.sum(weights, 0, keepdims=True)
        summed = weigh(prefix_turned, weights)

        def key_step(place, state):
            top, total, summed = state
            seen = same_pair(columns_ref[place, :], code_row)
            seen = jnp.concatenate([seen] * count, 1)
            scores = jnp.where(seen, dot(k_ref[place, :], rows), -jnp.inf)
            new_top = jnp.maximum(top, jnp.max(scores, 0, keepdims=True))
            factor = jnp.exp2(top - new_top)
            weights = jnp.exp2(scores - new_top)
            total = total * factor + jnp.sum(weights, 0, keepdims=True)
            summed = summed * factor + weigh(v_turned[:, place], weights)
            return new_top, total, summed

        low, high = low_ref[i], high_ref[i]
        twos = (high - low) // 2

        def two_blocks(j, state):
            start = pl.multiple_of((low + 2 * j) * BLOCK, BLOCK)
            return key_step(pl.ds(start, 2 * BLOCK), state)

        def one_block(j, state):
            return key_step(pl.ds(pl.multiple_of(j * BLOCK, BLOCK), BLOCK), state)

        state = lax.fori_loop(0, twos, two_blocks, (top, total, summed))
        top, total, summed = lax.fori_loop(low + 2 * twos, high, one_block, state)
        logs = top + jnp.log2(total)
        group_place = pl.ds(pl.multiple_of(i * group_lanes, group_lanes), group_lanes)
        for group in range(groups):
            lanes = slice(group * group_lanes, (group + 1) * group_lanes)
            total_ref[group, :, group_place] = logs[:, lanes]
        summed = summed / total
        turned = jnp.concatenate([summed[:, lanes_of(h)] for h in range(count)], 0)
        turned_ref[:, at] = turned
        context = turned.T.astype(jnp.bfloat16)
        share = min(BLOCK, own_rows)
        for part in range(BLOCK // share):
            first = i * BLOCK + part * share
            device, start = first // own_rows, first % own_rows
            for step, context_ref in enumerate(contexts):

                @pl.when(device ^ me == step)
                def _(context_ref=context_ref, start=start, part=part):
                    inside = pl.ds(pl.multiple_of(start, share), share)
                    context_ref[inside, :] = context[part * share : (part + 1) * share]

        return carry

    lax.fori_loop(0, blocks, query_step, 0)


def groups_of(width):
    return max(width // (2 * HEAD), 1)


def attend(low, high, me, tokens, matrix, bias, prefix_k, prefix_v, columns, row):
    devices = len(tokens) // 2
    rows = row.shape[1]
    width = prefix_k.shape[1]
    count = width // HEAD
    groups = groups_of(width)
    own_rows = rows // devices
    results = scalar_call(
        functools.partial(attend_kernel, count, devices),
        "attend",
        40,
        (low, high, me),
        (*tokens, matrix, bias, prefix_k, prefix_v, columns, row),
        [((own_rows, width), jnp.bfloat16)] * devices
        + [
            ((width, rows), jnp.float32),
            ((groups, 1, count // groups * rows), jnp.float32),
        ]
        + [((rows, width), jnp.bfloat16)] * 3,
        [pltpu.VMEM((width, rows), jnp.bfloat16)] * 2,
    )
    return results[:devices], results[devices:]


def attend_back_kernel(count, devices, low_ref, high_ref, me_ref, *refs):
    pieces, refs = refs[:devices], refs[devices:]
    (q_ref, k_ref, v_ref, pk_ref, pv_ref, turned_ref, total_ref, columns_ref, row_ref), refs = (
        refs[:9],
        refs[9:],
    )
    results, refs = refs[:devices], refs[devices:]
    prefix_ref, refs = refs[0], refs[1:]
    (
        g_ref,
        grads_ref,
        q_turned,
        g_turned,
        q_alone,
        g_alone,
        k_turned,
        q_sum,
        delta_ref,
        k_sum,
        v_sum,
        pk_sum,
        pv_sum,
    ) = refs
    me = me_ref[0]
    width = count * HEAD
    blocks = q_ref.shape[0] // BLOCK
    own_rows = pieces[0].shape[0]

    def rows_of(step):
        return pl.ds(pl.multiple_of((me ^ step) * own_rows, own_rows), own_rows)

    for step, piece_ref in enumerate(pieces):
        g_ref[rows_of(step), :] = piece_ref[...]
    k_turned[...] = k_ref[...].T
    prefix_turned = pk_ref[...].T
    q_sum[...] = jnp.zeros_like(q_sum)
    pk_sum[...] = jnp.zeros_like(pk_sum)
    pv_sum[...] = jnp.zeros_like(pv_sum)

    def wide(i):
        return pl.ds(pl.multiple_of(i * count * BLOCK, count * BLOCK), count * BLOCK)

    def query_part(i):
        return pl.ds(pl.multiple_of(i * BLOCK, BLOCK), BLOCK)

    def pair_of_blocks(i, keys, values, keys_turned, seen, key_total, value_total):
        at = query_part(i)
        scores = dot(keys, q_turned[:, wide(i)])
        grad_weights = dot(values, g_turned[:, wide(i)])
        weights = jnp.exp2(scores - total_ref[0, :, wide(i)])
        if seen is not None:
            seen = jnp.concatenate([same_pair(seen, row_ref[:, at])] * count, 1)
            weights = jnp.where(seen, weights, 0.0)
        grad_scores = weights * (grad_weights - delta_ref[:, wide(i)])
        grad_scores = grad_scores.astype(jnp.bfloat16)
        value_total[...] += dot(weights.astype(jnp.bfloat16), g_alone[wide(i), :])
        key_total[...] += dot(grad_scores, q_alone[wide(i), :])
        for h in range(count):
            q_sum[head_of(h), at] += dot(keys_turned[head_of(h)], grad_scores[:, lanes_of(h)])

    lane = lax.broadcasted_iota(jnp.int32, (1, width), 1)

    def prepare(i, carry):
        at = query_part(i)
        q_block = q_ref[at, :].T
        g_block = g_ref[at, :].T
        delta = g_block.astype(jnp.float32) * turned_ref[:, at]
        delta_ref[:, wide(i)] = jnp.concatenate(
            [jnp.sum(delta[head_of(h)], 0, keepdims=True) for h in range(count)], 1
        )
        q_apart, g_apart = heads_apart(q_block, count), heads_apart(g_block, count)
        q_turned[:, wide(i)] = q_apart
        g_turned[:, wide(i)] = g_apart
        for h in range(count):
            own = (lane // HEAD == h).astype(jnp.bfloat16)
            alone = pl.ds(pl.multiple_of((i * count + h) * BLOCK, BLOCK), BLOCK)
            q_alone[alone, :] = q_ref[at, :] * own
            g_alone[alone, :] = g_ref[at, :] * own
        pair_of_blocks(i, pk_ref[...], pv_ref[...], prefix_turned, None, pk_sum, pv_sum)
        return carry

    lax.fori_loop(0, blocks, prepare, 0)
    prefix_ref[0] = pk_sum[...] * LN_2
    prefix_ref[1] = pv_sum[...]

    def key_step(j, carry):
        place = pl.ds(pl.multiple_of(j * 4 * BLOCK, 4 * BLOCK), 4 * BLOCK)
        k_sum[...] = jnp.zeros_like(k_sum)
        v_sum[...] = jnp.zeros_like(v_sum)
        keys = k_ref[place, :]
        values = v_ref[place, :]
        keys_turned = k_turned[:, place]
        seen = columns_ref[place, :]

        def query_step(i, carry):
            pair_of_blocks(i, keys, values, keys_turned, seen, k_sum, v_sum)
            return carry

        lax.fori_loop(low_ref[4 * j], high_ref[4 * j + 3], query_step, 0)
        grads_ref[place, width : 2 * width] = (k_sum[...] * LN_2).astype(jnp.bfloat16)
        grads_ref[place, 2 * width :] = v_sum[...].astype(jnp.bfloat16)
        return carry

    lax.fori_loop(0, blocks // 4, key_step, 0)
    grads_ref[:, :width] = (q_sum[...] * SCALE).T.astype(jnp.bfloat16)
    for step, result_ref in enumerate(results):
        result_ref[...] = grads_ref[rows_of(step), :]


def attend_back(low, high, me, group, pieces, attended, prefix_k, prefix_v, columns, row):
    devices = len(pieces)
    turned, total, queries, keys, values = attended
    own_rows, all_width = pieces[0].shape
    rows, width = own_rows * devices, all_width // groups_of(all_width)
    prefix = prefix_k.shape[0]
    count = width // HEAD
    specs = {
        at: pl.BlockSpec((few, width), lambda t, *_: (0, group))
        for at, few in enumerate([own_rows] * devices + [rows, rows, rows, prefix, prefix])
    }
    specs[devices + 5] = pl.BlockSpec((width, rows), lambda t, *_: (group, 0))
    specs[devices + 6] = pl.BlockSpec((1, 1, total.shape[2]), lambda t, *_: (group, 0, 0))
    results = scalar_call(
        functools.partial(attend_back_kernel, count, devices),
        "attend_back",
        30,
        (low, high, me),
        (*pieces, queries, keys, values, prefix_k, prefix_v, turned, total, columns, row),
        [((rows // devices, 3 * width), jnp.bfloat16)] * devices
        + [((2, prefix, width), jnp.float32)],
        [
            pltpu.VMEM((rows, width), jnp.bfloat16),
            pltpu.VMEM((rows, 3 * width), jnp.bfloat16),
            pltpu.VMEM((width, count * rows), jnp.bfloat16),
            pltpu.VMEM((width, count * rows), jnp.bfloat16),
            pltpu.VMEM((count * rows, width), jnp.bfloat16),
            pltpu.VMEM((count * rows, width), jnp.bfloat16),
            pltpu.VMEM((width, rows), jnp.bfloat16),
            pltpu.VMEM((width, rows), jnp.float32),
            pltpu.VMEM((1, count * rows), jnp.float32),
            pltpu.VMEM((4 * BLOCK, width), jnp.float32),
            pltpu.VMEM((4 * BLOCK, width), jnp.float32),
            pltpu.VMEM((prefix, width), jnp.float32),
            pltpu.VMEM((prefix, width), jnp.float32),
        ],
        specs=specs,
    )
    return results[:devices], results[devices]


def own_block(me, step, size):
    return pl.ds(pl.multiple_of((me ^ step) * size, size), size)


def mix_kernel(devices, me_ref, *refs):
    contexts, refs = refs[:devices], refs[devices:]
    upper_ref, lower_ref, matrix_ref, bias_ref, normal_ref, inverse_ref = refs
    me = me_ref[0]
    width = contexts[0].shape[1]
    tokens = jnp.concatenate([upper_ref[...], lower_ref[...]], 0)
    total = tokens.astype(jnp.float32) + bias_ref[...]
    for step, context_ref in enumerate(contexts):
        total += dot(context_ref[...], matrix_ref[own_block(me, step, width), :])
    normal_ref[...], inverse_ref[...] = normalize(total)


def mix(me, contexts, upper, lower, matrix, bias):
    rows, width = contexts[0].shape[0], upper.shape[1]
    return scalar_call(
        functools.partial(mix_kernel, len(contexts)),
        "mix",
        5,
        (me,),
        (*contexts, upper, lower, matrix, bias),
        [((rows, width), jnp.float32), ((rows, 1), jnp.float32)],
        [],
    )


def copy_in(sources, targets, sems):
    copies = [
        pltpu.make_async_copy(source, target, sems.at[at])
        for at, (source, target) in enumerate(zip(sources, targets, strict=True))
    ]
    for item in copies:
        item.start()
    return copies


def feed_kernel(parts, pieces, me_ref, core_ref, *refs):
    in_refs, back_refs, refs = refs[:parts], refs[parts : 2 * parts], refs[2 * parts :]
    (normal_ref, gain_one, shift_one, bias_in, bias_back, gain_two, shift_two), refs = (
        refs[:7],
        refs[7:],
    )
    outputs, refs = refs[:pieces], refs[pieces:]
    slope_ref, normal_two, inverse_two, held, total, in_held, back_held, slope_held = refs[:8]
    in_sems, back_sems, slope_sems = refs[8:]
    hidden = in_held.shape[2]
    in_copies, back_copies = [], []
    for t in range(parts):
        one = slice(t, t + 1)
        in_copies += copy_in(in_refs[one], [in_held.at[t]], in_sems.at[one])
        back_copies += copy_in(back_refs[one], [back_held.at[t]], back_sems.at[one])
    normed = normal_ref[...] * gain_one[...] + shift_one[...]
    held[...] = normed.astype(jnp.bfloat16)
    total[...] = normed + bias_back[...]

    def inner_of(t):
        in_copies[t].wait()
        back_copies[t].wait()
        bias = bias_in[(t % 2) ^ core_ref[0], me_ref[0] ^ (t // 2)]
        return dot(held[...], in_held[t]) + bias

    slopes = []
    following = inner_of(0)
    for t in range(parts):
        inner = following
        if t + 1 < parts:
            following = inner_of(t + 1)
        activated, slope = gelu_pair(inner)
        slope_held[t] = slope.astype(jnp.bfloat16)
        target = slope_ref.at[:, t * hidden : (t + 1) * hidden]
        slopes.append(pltpu.make_async_copy(slope_held.at[t], target, slope_sems.at[t]))
        slopes[-1].start()
        total[...] += dot(activated.astype(jnp.bfloat16), back_held[t])
    normal, inverse = normalize(total[...])
    normal_two[...] = normal
    inverse_two[...] = inverse
    result = (normal * gain_two[...] + shift_two[...]).astype(jnp.bfloat16)
    size = result.shape[0] // pieces
    for at, output_ref in enumerate(outputs):
        output_ref[...] = result[at * size : (at + 1) * size]
    for item in slopes:
        item.wait()


def feed(me, core, ins, backs, normal, gain_one, shift_one, bias_in, bias_back, gain_two, shift_two, pieces):
    parts = len(ins)
    rows, width = normal.shape
    hidden = ins[0].shape[1]
    anywhere = pl.BlockSpec(memory_space=pl.ANY)
    results = scalar_call(
        functools.partial(feed_kernel, parts, pieces),
        "feed",
        22,
        (me, core),
        (*ins, *backs, normal, gain_one, shift_one, bias_in, bias_back, gain_two, shift_two),
        [((rows // pieces, width), jnp.bfloat16)] * pieces
        + [
            ((rows, parts * hidden), jnp.bfloat16),
            ((rows, width), jnp.float32),
            ((rows, 1), jnp.float32),
        ],
        [
            pltpu.VMEM((rows, width), jnp.bfloat16),
            pltpu.VMEM((rows, width), jnp.float32),
            pltpu.VMEM((parts, width, hidden), jnp.bfloat16),
            pltpu.VMEM((parts, hidden, width), jnp.bfloat16),
            pltpu.VMEM((parts, rows, hidden), jnp.bfloat16),
            pltpu.SemaphoreType.DMA((parts,)),
            pltpu.SemaphoreType.DMA((parts,)),
            pltpu.SemaphoreType.DMA((parts,)),
        ],
        specs={at: anywhere for at in range(2 * parts)},
        outs={pieces: anywhere},
    )
    return results[:pieces], results[pieces:]


def collect_copies(pieces, matrix_ref, grad_ref, held):
    piece_held, matrix_held, grad_held, piece_sems, matrix_sems, grad_sem = held
    width = pieces[0].shape[1]
    every = range(len(pieces))
    grad_copy = pltpu.make_async_copy(grad_ref, grad_held, grad_sem.at[0])
    piece_copies, matrix_copies = [], []
    for at in every:
        piece_copies += copy_in([pieces[at]], [piece_held.at[at]], piece_sems.at[at : at + 1])
        if matrix_held.shape[0] > at:
            block = matrix_ref
            if matrix_held.shape[0] > 1:
                block = matrix_ref.at[:, at * width : (at + 1) * width]
            matrix_copies += copy_in([block], [matrix_held.at[at]], matrix_sems.at[at : at + 1])
    grad_copy.start()
    return grad_copy, piece_copies, matrix_copies


def collect_held(copies, held):
    grad_copy, piece_copies, matrix_copies = copies
    total = None
    width = held[0].shape[2]
    for at, piece_copy in enumerate(piece_copies):
        piece_copy.wait()
        if at < len(matrix_copies):
            matrix_copies[at].wait()
        if len(matrix_copies) > 1:
            block = held[1][at]
        else:
            block = held[1][0, :, at * width : (at + 1) * width]
        product = back_dot(held[0][at], block)
        total = product if total is None else total + product
    grad_copy.wait()
    return total + held[2][...]


def collect_scratch(pieces, matrix, grad):
    count = len(pieces)
    rows, width = pieces[0].shape
    blocks = 1 if width % 128 else count
    return [
        pltpu.VMEM((count, rows, width), jnp.bfloat16),
        pltpu.VMEM((blocks, matrix.shape[0], matrix.shape[1] // blocks), jnp.bfloat16),
        pltpu.VMEM(grad.shape, grad.dtype),
        pltpu.SemaphoreType.DMA((count,)),
        pltpu.SemaphoreType.DMA((count,)),
        pltpu.SemaphoreType.DMA((1,)),
    ]


def collect_kernel(count, *refs):
    pieces, (matrix_ref, grad_ref, result_ref), held = refs[:count], refs[count : count + 3], refs[count + 3 :]
    copies = collect_copies(pieces, matrix_ref, grad_ref, held)
    result_ref[...] = collect_held(copies, held).astype(result_ref.dtype)


def collect(pieces, matrix, grad):
    return scalar_call(
        functools.partial(collect_kernel, len(pieces)),
        "collect",
        9,
        (),
        (*pieces, matrix, grad),
        [(grad.shape, jnp.bfloat16)],
        collect_scratch(pieces, matrix, grad),
        specs={at: pl.BlockSpec(memory_space=pl.ANY) for at in range(len(pieces) + 2)},
    )[0]


def feed_back_kernel(parts, devices, count, me_ref, *refs):
    in_refs, back_refs, refs = refs[:parts], refs[parts : 2 * parts], refs[2 * parts :]
    (
        slope_ref,
        normal_one,
        matrix_ref,
    ), refs = refs[:3], refs[3:]
    behind, refs = refs[: max(count + 2, 1)], refs[max(count + 2, 1) :]
    (normal_two, inverse_two, gain_two, inverse_one, gain_one), refs = refs[:5], refs[5:]
    grad_one_ref, refs = refs[0], refs[1:]
    results, refs = refs[:devices], refs[devices:]
    held, total, in_held, back_held, slope_held, normal_held, matrix_held = refs[:7]
    in_sems, back_sems, slope_sems, late_sems = refs[7:11]
    hidden = in_held.shape[2]
    if count > 0:
        collected = collect_copies(behind[:count], behind[count], behind[count + 1], refs[11:])
    back_copies, slope_copies, in_copies = [], [], []
    for t in range(parts):
        one = slice(t, t + 1)
        slope_part = slope_ref.at[:, t * hidden : (t + 1) * hidden]
        back_copies += copy_in(back_refs[one], [back_held.at[t]], back_sems.at[one])
        slope_copies += copy_in([slope_part], [slope_held.at[t]], slope_sems.at[one])
        in_copies += copy_in(in_refs[one], [in_held.at[t]], in_sems.at[one])
    late_copies = copy_in([normal_one, matrix_ref], [normal_held, matrix_held], late_sems)
    if count > 0:
        gradient = collect_held(collected, refs[11:])
    else:
        gradient = behind[0][...].astype(jnp.float32)
    grad_two = normalize_back(gradient, normal_two[...], inverse_two[...], gain_two[...])
    held[...] = grad_two.astype(jnp.bfloat16)
    total[...] = grad_two

    def inner_of(t):
        back_copies[t].wait()
        slope_copies[t].wait()
        in_copies[t].wait()
        return back_dot(held[...], back_held[t])

    following = inner_of(0)
    for t in range(parts):
        inner = following
        if t + 1 < parts:
            following = inner_of(t + 1)
        grad_inner = (inner * slope_held[t].astype(jnp.float32)).astype(jnp.bfloat16)
        total[...] += back_dot(grad_inner, in_held[t])
    for item in late_copies:
        item.wait()
    grad_one = normalize_back(total[...], normal_held[...], inverse_one[...], gain_one[...])
    grad_one_ref[...] = grad_one
    rounded = grad_one.astype(jnp.bfloat16)
    size = results[0].shape[1]
    for step, result_ref in enumerate(results):
        product = back_dot(rounded, matrix_held[own_block(me_ref[0], step, size), :])
        result_ref[...] = product.astype(jnp.bfloat16)


def feed_back(me, devices, ins, backs, behind, slope, norms, gain_two, gain_one, matrix):
    normal_one, inverse_one, normal_two, inverse_two = norms
    parts = len(ins)
    rows, width = normal_one.shape
    count = len(behind) - 2
    hidden = ins[0].shape[1]
    anywhere = pl.BlockSpec(memory_space=pl.ANY)
    results = scalar_call(
        functools.partial(feed_back_kernel, parts, devices, count),
        "feed_back",
        18,
        (me,),
        (
            *ins,
            *backs,
            slope,
            normal_one,
            matrix,
            *behind,
            normal_two,
            inverse_two,
            gain_two,
            inverse_one,
            gain_one,
        ),
        [((rows, width), jnp.float32)]
        + [((rows, width // devices), jnp.bfloat16)] * devices,
        [
            pltpu.VMEM((rows, width), jnp.bfloat16),
            pltpu.VMEM((rows, width), jnp.float32),
            pltpu.VMEM((parts, width, hidden), jnp.bfloat16),
            pltpu.VMEM((parts, hidden, width), jnp.bfloat16),
            pltpu.VMEM((parts, rows, hidden), jnp.bfloat16),
            pltpu.VMEM(normal_one.shape, normal_one.dtype),
            pltpu.VMEM(matrix.shape, matrix.dtype),
            pltpu.SemaphoreType.DMA((parts,)),
            pltpu.SemaphoreType.DMA((parts,)),
            pltpu.SemaphoreType.DMA((parts,)),
            pltpu.SemaphoreType.DMA((2,)),
        ]
        + (collect_scratch(behind[:count], behind[count], behind[count + 1]) if count > 0 else []),
        specs={at: anywhere for at in range(2 * parts + 3 + (count + 2 if count > 0 else 0))},
    )
    return results[0], results[1:]


def local(
    dp_count,
    seq_count,
    first_layer_input,
    cotangent,
    lengths,
    w_qkv,
    bias_qkv,
    w_out,
    bias_out,
    w_in,
    bias_in,
    w_back,
    bias_back,
    norm_gain,
    norm_shift,
    prefix_keys,
    prefix_values,
):
    row_count = first_layer_input.shape[1]
    width = first_layer_input.shape[2]
    layer_count = w_qkv.shape[0]
    hidden = w_in.shape[2]
    all_rows = row_count * seq_count
    own_width = width // seq_count
    me = lax.axis_index("seq")
    core = lax.axis_index("dp") % 2
    me_at = me[None].astype(jnp.int32)
    core_at = core[None].astype(jnp.int32)
    bits = [1 << n for n in range(seq_count.bit_length() - 1)]

    def swap(value, step):
        return lax.ppermute(value, "seq", [(i, i ^ step) for i in range(seq_count)])

    def widen(found, order):
        for bit in order:
            found = found | {
                k | bit: swap(item, bit) for k, item in found.items() if k | bit not in found
            }
        return found

    def exchange(value, order):
        found = widen({0: value}, order)
        return [found[k] for k in range(seq_count)]

    def other_core(value):
        return lax.ppermute(value, "dp", [(i, i ^ 1) for i in range(dp_count)])

    def gather(value):
        return lax.all_gather(value, "dp", axis=0, tiled=True)

    def own_columns(values, axis):
        return lax.dynamic_slice_in_dim(values, me * own_width, own_width, axis)

    pair_at = jnp.arange(lengths.shape[1], dtype=jnp.int32)
    ends = jnp.sum(
        jnp.where(pair_at[:, None] <= pair_at[None, :], lengths[0][:, None], 0), 0, dtype=jnp.int32
    )
    starts = ends - lengths[0]
    places = jnp.arange(all_rows, dtype=jnp.int32)
    codes = jnp.sum((places[:, None] >= ends[None, :]).astype(jnp.int32), 1, dtype=jnp.int32)
    columns = jnp.broadcast_to(codes[:, None], (all_rows, 128))
    row = codes[None, :]
    first = jnp.arange(all_rows // BLOCK, dtype=jnp.int32) * BLOCK
    after = first + BLOCK
    low = jnp.max(jnp.where(starts[None, :] <= first[:, None], starts[None, :], 0), 1) // BLOCK
    high = jnp.min(jnp.where(ends[None, :] >= after[:, None], ends[None, :], all_rows), 1)
    high = (high + BLOCK - 1) // BLOCK

    groups = groups_of(own_width)
    half_rows = row_count // 2
    upper, lower = first_layer_input[0, :half_rows], first_layer_input[0, half_rows:]
    first_tokens = exchange(upper, bits), exchange(lower, bits[::-1])

    share = hidden // dp_count // seq_count

    def after(value, *others):
        return lax.optimization_barrier((value, *others))[0]

    def own_qkv(matrix):
        shard = matrix.reshape(-1, 3, seq_count, own_width)
        return lax.dynamic_slice_in_dim(shard, me, 1, 2).reshape(-1, 3 * own_width)

    def all_qkv(matrix):
        shard = matrix.reshape(-1, 3, seq_count, groups, own_width // groups)
        shard = jnp.transpose(shard, (2, 0, 3, 1, 4))
        blocks = [lax.dynamic_slice_in_dim(shard, me ^ step, 1, 0)[0] for step in range(seq_count)]
        return jnp.concatenate([block.reshape(-1, 3 * own_width) for block in blocks], 1)

    def hidden_share(into, back):
        into = into.reshape(-1, dp_count, seq_count, share)
        into = lax.dynamic_slice_in_dim(into, me, 1, 2).reshape(-1, dp_count * share)
        back = lax.dynamic_slice_in_dim(back, me * share, share, 0).reshape(into.shape)
        both = lax.all_gather(jnp.stack([into, back]), "dp")
        into = both[:, 0].reshape(width, dp_count * share)
        back = both[:, 1].reshape(dp_count * share, width)
        return into, back

    def hidden_first(into, back, both):
        half = dp_count * share // 2
        ins, backs = (
            [
                lax.dynamic_slice_in_dim(item, side * half, half, axis)
                for side in (core, 1 - core)
            ]
            for item, axis in ((into, 1), (back, 0))
        )
        in_found, back_found = {0: ins[0]}, {0: backs[0]}
        for bit in bits if both else bits[:1]:
            in_found[bit] = swap(ins[0], bit)
        for bit in bits if both else bits[-1:]:
            back_found[bit] = swap(backs[0], bit)
        return ins[1], backs[1], in_found, back_found

    def hidden_rest(in_other, back_other, in_found, back_found):
        return in_other, back_other, widen(in_found, bits), widen(back_found, bits[::-1])

    def hidden_all(in_other, back_other, in_found, back_found):
        ins, backs = [in_found[0], in_other], [back_found[0], back_other]
        for step in range(1, seq_count):
            ins += [in_found[step], other_core(in_found[step])]
            backs += [back_found[step], other_core(back_found[step])]
        return ins, backs

    def row_of(values):
        return values.astype(jnp.float32)[None, :]

    def over_dp_swap(value, bit):
        return lax.ppermute(value, "dp", [(i, i ^ bit) for i in range(dp_count)])

    saved = []
    tokens = first_tokens
    shares = [hidden_share(w_in[0], w_back[0])]
    mat_own = [gather(own_qkv(w_qkv[0]))]
    came = [found[bit] for found in first_tokens for bit in bits]
    mat_outs = [gather(after(w_out[0], came))]
    for layer in range(1, layer_count):
        shares.append(hidden_share(*after((w_in[layer], w_back[layer]), tokens)))
        mat_own.append(gather(own_qkv(after(w_qkv[layer], tokens))))
        mat_outs.append(gather(after(w_out[layer], tokens)))
    parts = hidden_first(*shares[0], True)
    for layer in range(layer_count):
        last = layer + 1 == layer_count
        bias_own = own_columns(bias_qkv[layer].reshape(3, width).astype(jnp.float32), 1)
        bias_own = bias_own.reshape(1, 3 * own_width)
        prefix_k = own_columns(prefix_keys[layer], 1)
        prefix_v = own_columns(prefix_values[layer], 1)
        bias_hidden = bias_in[layer].astype(jnp.float32).reshape(2, dp_count // 2, seq_count, share)
        bias_hidden = jnp.transpose(bias_hidden, (0, 2, 1, 3)).reshape(2, seq_count, 1, -1)
        tokens = [item for pair in zip(*tokens, strict=True) for item in pair]
        contexts, attended = attend(
            low, high, me_at, tokens, mat_own[layer], bias_own, prefix_k, prefix_v, columns, row
        )
        if layer:
            parts = hidden_rest(*parts)
            contexts = after(contexts, parts)
        else:
            contexts = after(contexts, parts)
            parts = hidden_rest(*parts)
        contexts = [contexts[0]] + [swap(contexts[k], k) for k in range(1, seq_count)]
        ins, backs = hidden_all(*parts)
        normal_one, inverse_one = mix(
            me_at, contexts, upper, lower, mat_outs[layer], row_of(bias_out[layer])
        )
        if not last:
            parts = hidden_first(*shares[layer + 1], False)
        outputs, (slope, normal_two, inverse_two) = feed(
            me_at,
            core_at,
            ins,
            backs,
            normal_one,
            row_of(norm_gain[layer, 0]),
            row_of(norm_shift[layer, 0]),
            bias_hidden,
            row_of(bias_back[layer]),
            row_of(norm_gain[layer, 1]),
            row_of(norm_shift[layer, 1]),
            1 if last else 2,
        )
        saved.append(
            (
                (attended, prefix_k, prefix_v),
                (normal_one, inverse_one, normal_two, inverse_two),
                (ins, backs, slope, mat_outs[layer]),
            )
        )
        if last:
            hidden_out = outputs[0]
        else:
            upper, lower = after(outputs, parts)
            tokens = exchange(upper, bits), exchange(lower, bits[::-1])
            if not layer:
                mat_qkv = [gather(all_qkv(after(matrix, upper))) for matrix in w_qkv]

    def over_dp(own):
        stride = 1
        while stride < dp_count:
            own = own + over_dp_swap(own, stride)
            stride *= 2
        return own

    behind = [cotangent[0]]
    prefix_grads = []
    for layer in reversed(range(layer_count)):
        (attended, prefix_k, prefix_v), norms, (ins, backs, slope, mat_out) = saved[layer]
        grad_one, pieces = feed_back(
            me_at,
            seq_count,
            ins,
            backs,
            behind,
            slope,
            norms,
            row_of(norm_gain[layer, 1]),
            row_of(norm_gain[layer, 0]),
            mat_out,
        )
        pieces = [pieces[0]] + [swap(pieces[k], k) for k in range(1, seq_count)]
        grads, layer_grads = [], []
        for group in range(groups):
            found, prefix_grad = attend_back(
                low,
                high,
                me_at,
                group,
                pieces,
                attended,
                prefix_k,
                prefix_v,
                columns,
                row,
            )
            layer_grads.append(prefix_grad)
            if grads:
                found = after(found, grads[-1])
            elif prefix_grads:
                found = after(found, prefix_grads[-1])
            grads.append([found[0]] + [swap(found[k], k) for k in range(1, seq_count)])
        layer_grads = over_dp(jnp.concatenate(layer_grads, 2))
        layer_grads = after(layer_grads, grads[-1])
        prefix_grads.append([layer_grads] + [swap(layer_grads, k) for k in range(1, seq_count)])
        grads = [grads[group][k] for k in range(seq_count) for group in range(groups)]
        behind = [*grads, mat_qkv[layer], grad_one]
    gradient = collect(behind[:-2], *behind[-2:])

    found = [jnp.stack(items) for items in zip(*prefix_grads[::-1], strict=True)]
    for bit in bits:
        found = [jnp.where(me & bit, found[k ^ bit], found[k]) for k in range(seq_count)]
    whole = jnp.concatenate(found, 3)
    return (hidden_out[None], gradient[None], whole[:, 0], whole[:, 1])


def solution(mesh):
    in_specs = (
        P("dp", "seq", None),
        P("dp", "seq", None),
        P("dp", None),
        P(None, "dp", None),
        P(),
        P(None, "dp", None),
        P(),
        P(None, "dp", None),
        P(),
        P(None, "dp", None),
        P(),
        P(),
        P(),
        P(),
        P(),
    )
    out_specs = (P("dp", "seq", None), P("dp", "seq", None), P(), P())
    return jax.shard_map(
        functools.partial(local, mesh.shape["dp"], mesh.shape["seq"]),
        mesh=mesh,
        in_specs=in_specs,
        out_specs=out_specs,
        check_vma=False,
    )
```
